256 devices in a mesh: lat: 8 (over z), lon: 32 (over x, y, core).
Axes of the slice: x: 4, y: 4, z: 8, core: 2. Of those that a mesh axis runs over, the one named last changes fastest.
Arguments:
- ensemble: float32 [256, 512, 8, 256], P('lat', 'lon'), may hold values from -6 to 6
- obs_values: float32 [3, 256], replicated, may hold values from -8 to 8
- obs_noise: float32 [3, 256, 256], replicated, may hold values from -6 to 6
- obs_var: float32 [3, 256], replicated, may hold values from 0.1 to 1
- obs_cells: int32 [3, 256], replicated, may hold values from 0 to 4095, as said below
- owner_tiles: int32 [3, 2], replicated, may hold values from 0 to 31, as said below
- radius: int32 [3], replicated, may hold values from 64 to 128, as said below
- courant_lat: float32 [256, 512, 8], P('lat', 'lon'), may hold values from -0.35 to 0.35
- courant_lon: float32 [256, 512, 8], P('lat', 'lon'), may hold values from -0.35 to 0.35
- diffusivity: float32 [256, 512, 8], P('lat', 'lon'), may hold values from 0.02 to 0.07
Outputs:
- forecast: float32 [256, 512, 8, 256], P('lat', 'lon')
The draws below stay inside these ranges and needn't reach their ends.
Inputs may be any that keep to these rules, and one draw needn't show every extreme that they name: `obs_cells`: each row holds 256 distinct local cells, the last cell of the tile among them; cell (i, j, k) of a tile has index (i * 16 + j) * 8 + k. `owner_tiles`: row b names a latitude tile below 8 and a longitude tile below 32; consecutive batches' tiles differ by at most one in each (longitude wraps). `radius`: every draw holds both ends.
All inputs are finite; a program needn't handle non-finite values.
Results may differ from the reference program's by a relative error of at most 0.0003.
Values sent between devices are 32-bit elements; how exact they have to be, the bound alone decides.
A program may use at most 64 MiB of HBM per device.

```python
import math
import jax
import jax.numpy as jnp
from jax import lax

MEMBERS = 256
LEV = 8
NOBS = 256
NBATCH = 3
CLAT = 32
CLON = 16
NLAT = 256
NLON = 512
RMIN = 64
RMAX = 128


def draw_ensemble(key, part):
    freq_key, coef_key, rough_key, phase_key = jax.random.split(jax.random.fold_in(key, 17), 4)
    mode_count = 24
    frequency = jax.random.uniform(freq_key, (mode_count, 3), jnp.float32, -1.5, 1.5)
    phase_shift = jax.random.uniform(phase_key, (mode_count,), jnp.float32, -3.14159, 3.14159)
    member_coef = jax.random.normal(coef_key, (mode_count, MEMBERS), jnp.float32)
    lat_place = (jnp.arange(NLAT, dtype=jnp.float32) / CLAT)[:, None, None]
    lon_place = (jnp.arange(NLON, dtype=jnp.float32) / CLON)[None, :, None]
    lev_place = (jnp.arange(LEV, dtype=jnp.float32) / LEV)[None, None, :]
    full_shape = (NLAT, NLON, LEV, MEMBERS)
    smooth = jnp.zeros(full_shape, jnp.float32)
    for mode_index in range(mode_count):
        phase_angle = 6.2831853 * (frequency[mode_index, 0] * lat_place + frequency[mode_index, 1] * lon_place + frequency[mode_index, 2] * lev_place) + phase_shift[mode_index]
        amplitude = 0.81 * 0.82 ** mode_index
        smooth = smooth + (amplitude * jnp.sin(phase_angle))[..., None] * member_coef[mode_index]
    rough_part = 0.8 * jax.random.normal(rough_key, full_shape, jnp.float32)
    return jnp.clip(smooth + rough_part, -6.0, 6.0).astype(jnp.float32)


def draw_obs_cells(key, part):
    keys = jax.random.split(jax.random.fold_in(key, 7), NBATCH)
    last_cell = CLAT * CLON * LEV - 1
    picked = []
    for index in range(NBATCH):
        chosen = jax.random.permutation(keys[index], last_cell)[:NOBS - 1]
        picked.append(jnp.concatenate([chosen.astype(jnp.int32), jnp.full((1,), last_cell, jnp.int32)]))
    return jnp.stack(picked).astype(jnp.int32)


def draw_owner_tiles(key, part):
    first_key, second_key, third_key = jax.random.split(jax.random.fold_in(key, 11), 3)
    lon_tiles = NLON // CLON
    lat_anchor = jax.random.randint(first_key, (), 0, NBATCH).astype(jnp.int32)
    lon_anchor = jax.random.randint(second_key, (), 0, NBATCH).astype(jnp.int32)
    moves = jax.random.randint(third_key, (NBATCH, 2), -1, 2).astype(jnp.int32)
    moves = moves.at[0].set(jnp.zeros((2,), jnp.int32))
    walked = jnp.cumsum(moves, axis=0).astype(jnp.int32)
    lat_walk = walked[:, 0]
    lon_walk = walked[:, 1]
    lat_tile = jnp.abs(lat_walk - lat_walk[lat_anchor])
    lon_tile = (lon_tiles - 1 + lon_walk - lon_walk[lon_anchor] + 4 * lon_tiles) % lon_tiles
    return jnp.stack([lat_tile, lon_tile], axis=1).astype(jnp.int32)


def draw_radius(key, part):
    first_key, second_key = jax.random.split(jax.random.fold_in(key, 13), 2)
    middle = jax.random.randint(first_key, (), RMIN, RMAX + 1)
    order = jax.random.permutation(second_key, 3)
    listed = jnp.stack([jnp.asarray(RMAX, jnp.int32), jnp.asarray(RMIN, jnp.int32), middle.astype(jnp.int32)])
    return listed[order].astype(jnp.int32)


def block_scale(stream_key, dims, cuts, smallest, largest):
    def one(dim, shards_of):
        steps = jax.random.uniform(jax.random.fold_in(jax.random.fold_in(stream_key, 6), dim), (shards_of,), jnp.float32, smallest / len(cuts), largest / len(cuts))
        return jnp.repeat(jnp.exp(steps), dims[dim] // shards_of).reshape((-1,) + (1,) * (len(dims) - dim - 1))

    factor_of = one(*cuts[0])
    for cut in cuts[1:]:
        factor_of = factor_of * one(*cut)
    return factor_of


def normal_values(rng, dims, scale, most, kind=jnp.bfloat16):
    drawn = jax.random.normal(rng, dims, jnp.float32) * scale
    return jnp.minimum(jnp.maximum(drawn, -most), most).astype(kind)


def setup_inputs(seed: int = 0) -> dict:
    arg_keys = jax.random.split(jax.random.key(seed), 11)
    return {
        "ensemble": draw_ensemble(jax.random.fold_in(arg_keys[10], 71), 0),
        "obs_values": normal_values(arg_keys[1], (NBATCH, NOBS), 1.5, 8.0, jnp.float32),
        "obs_noise": normal_values(arg_keys[2], (NBATCH, NOBS, MEMBERS), 1.0, 6.0, jnp.float32),
        "obs_var": jnp.clip(jnp.exp(jax.random.uniform(arg_keys[3], (NBATCH, NOBS), jnp.float32, math.log(0.1), math.log(1.0))), 0.1, 1.0),
        "obs_cells": draw_obs_cells(jax.random.fold_in(arg_keys[10], 71), 0),
        "owner_tiles": draw_owner_tiles(jax.random.fold_in(arg_keys[10], 71), 0),
        "radius": draw_radius(jax.random.fold_in(arg_keys[10], 71), 0),
        "courant_lat": jnp.clip(jax.random.uniform(arg_keys[7], (NLAT, NLON, LEV), jnp.float32, -0.35, 0.35) * block_scale(arg_keys[7], (NLAT, NLON, LEV), ((0, 8), (1, 32)), -0.4, 0.0), -0.35, 0.35),
        "courant_lon": jnp.clip(jax.random.uniform(arg_keys[8], (NLAT, NLON, LEV), jnp.float32, -0.35, 0.35) * block_scale(arg_keys[8], (NLAT, NLON, LEV), ((0, 8), (1, 32)), -0.4, 0.0), -0.35, 0.35),
        "diffusivity": jnp.clip(jnp.exp(math.log(0.07) - 1.252763 * jax.random.uniform(arg_keys[9], (NLAT, NLON, LEV), jnp.float32) ** block_scale(arg_keys[9], (NLAT, NLON, LEV), ((0, 8), (1, 32)), -0.2, 0.2)), 0.02, 0.07),
    }


def taper_weight(dist_sq, radius_cells):
    ratio = 1.0 - dist_sq / (radius_cells * radius_cells)
    return jnp.square(jnp.maximum(ratio, 0.0))

def analysis(observed_rows, values, noise, variance):
    members = observed_rows.shape[1]
    spread = observed_rows - lax.optimization_barrier(jnp.mean(observed_rows, axis=1, keepdims=True))
    covariance = jnp.dot(spread, spread.T, precision=lax.Precision.HIGHEST) / (members - 1) + jnp.diag(variance)
    innovation = values[:, None] + jnp.sqrt(variance)[:, None] * noise - observed_rows
    factor = jnp.linalg.cholesky(covariance)
    inner = jax.scipy.linalg.solve_triangular(factor, innovation, lower=True)
    weights = jax.scipy.linalg.solve_triangular(factor, inner, lower=True, trans=1)
    return (spread, weights)

def locality(lat_cells, lon_cells, cells, owner_lat, owner_lon, radius_cells, total_lon):
    position = cells // LEV
    obs_lat = owner_lat * CLAT + position // CLON
    obs_lon = owner_lon * CLON + position % CLON
    lat_gap = (lat_cells[:, None] - obs_lat[None, :]).astype(jnp.float32)
    lon_gap = jnp.abs(lon_cells[:, None] - obs_lon[None, :])
    lon_gap = jnp.minimum(lon_gap, total_lon - lon_gap).astype(jnp.float32)
    dist_sq = jnp.square(lat_gap) + jnp.square(lon_gap)
    return taper_weight(dist_sq, radius_cells.astype(jnp.float32))

def regress(flat_state, spread, weights, weight_map):
    members = flat_state.shape[1]
    places = weight_map.shape[0]
    levels = flat_state.shape[0] // places
    anomaly = flat_state - lax.optimization_barrier(jnp.mean(flat_state, axis=1, keepdims=True))
    covar = jnp.dot(anomaly, spread.T, precision=lax.Precision.HIGHEST) / (members - 1)
    covar = (covar.reshape(places, levels, -1) * weight_map[:, None, :]).reshape(covar.shape)
    return flat_state + jnp.dot(covar, weights, precision=lax.Precision.HIGHEST)

def advance(padded, lat_speed, lon_speed, spread_rate):
    centre = padded[1:-1, 1:-1]
    below_row = padded[:-2, 1:-1]
    above_row = padded[2:, 1:-1]
    west_col = padded[1:-1, :-2]
    east_col = padded[1:-1, 2:]
    lat_part = lat_speed[..., None]
    lon_part = lon_speed[..., None]
    rate_part = spread_rate[..., None]
    transport = jnp.maximum(lat_part, 0.0) * (centre - below_row) + jnp.minimum(lat_part, 0.0) * (above_row - centre) + jnp.maximum(lon_part, 0.0) * (centre - west_col) + jnp.minimum(lon_part, 0.0) * (east_col - centre)
    return centre - transport + rate_part * (below_row + above_row + west_col + east_col - 4.0 * centre)

def pad_global(field):
    padded = jnp.pad(field, ((1, 1), (0, 0), (0, 0)))
    return jnp.concatenate([padded[:, -1:], padded, padded[:, :1]], axis=1)

def reference(ensemble, obs_values, obs_noise, obs_var, obs_cells, owner_tiles, radius, courant_lat, courant_lon, diffusivity):
    nlat_all, nlon_all, levels, members = ensemble.shape
    state = ensemble
    zero_index = jnp.zeros((), jnp.int32)
    for which_batch in range(NBATCH):
        owner_lat = owner_tiles[which_batch, 0]
        owner_lon = owner_tiles[which_batch, 1]
        start_lat = (owner_lat * CLAT).astype(jnp.int32)
        start_lon = (owner_lon * CLON).astype(jnp.int32)
        owner_block = lax.dynamic_slice(state, (start_lat, start_lon, zero_index, zero_index), (CLAT, CLON, levels, members))
        observed_rows = owner_block.reshape(-1, members)[obs_cells[which_batch]]
        spread, weights = analysis(observed_rows, obs_values[which_batch], obs_noise[which_batch], obs_var[which_batch])
        cells = obs_cells[which_batch]
        reach = radius[which_batch]

        def one_row(packed):
            lat_row, lat_number = packed
            lat_cells = jnp.full((nlon_all,), lat_number, jnp.int32)
            lon_cells = jnp.arange(nlon_all, dtype=jnp.int32)
            weight_map = locality(lat_cells, lon_cells, cells, owner_lat, owner_lon, reach, nlon_all)
            return regress(lat_row.reshape(-1, members), spread, weights, weight_map).reshape(lat_row.shape)
        state = lax.map(one_row, (state, jnp.arange(nlat_all, dtype=jnp.int32)))
    by_level = jnp.moveaxis(state, 2, 0)
    coefs = (jnp.moveaxis(courant_lat, 2, 0), jnp.moveaxis(courant_lon, 2, 0), jnp.moveaxis(diffusivity, 2, 0))

    def one_level(packed):
        field, lat_speed, lon_speed, spread_rate = packed
        field = advance(pad_global(field), lat_speed, lon_speed, spread_rate)
        return advance(pad_global(field), lat_speed, lon_speed, spread_rate)
    moved = lax.map(one_level, (by_level,) + coefs)
    return jnp.moveaxis(moved, 0, 2)
```

```python
import functools

import jax
import jax.numpy as jnp
from jax import lax
from jax.experimental import pallas as pl
from jax.experimental.pallas import tpu as pltpu
from jax.sharding import PartitionSpec as P

F32 = jnp.float32
BF16 = jnp.bfloat16
HI = lax.Precision.HIGHEST
MESH = pl.DeviceIdType.MESH
NN = (((1,), (0,)), ((), ()))
NT = (((1,), (1,)), ((), ()))
TN = (((0,), (0,)), ((), ()))

LEV = 8
NB = 3
CLAT = 32
CLON = 16
NOBS = 256
MEM = 256
PIV = 4
PANEL = 32
VM = pltpu.VMEM
SM = pltpu.SMEM


def pick_kernel(cells_ref, own_ref, state_ref, out_ref):
    for b in range(NB):
        own = own_ref[b]

        def body(o, carry):
            for u in range(8):
                c = cells_ref[b, o * 8 + u]
                out_ref[b, pl.ds(o * 8 + u, 1), :] = state_ref[pl.ds(c, 1), :] * own
            return carry

        lax.fori_loop(0, NOBS // 8, body, 0)


def exchange_kernel(
    nlat,
    nlon,
    picked,
    edges,
    ens,
    rows,
    edges_in,
    ext,
    got1,
    got2,
    part1,
    part2,
    s1,
    r1,
    s2,
    r2,
    s3,
    r3,
    hs,
    hr,
    es,
    er,
    loc,
):
    l = lax.axis_index("lat")
    n = lax.axis_index("lon")
    piece = NOBS // nlon
    lm, lp = lax.rem(l + nlat - 1, nlat), lax.rem(l + 1, nlat)
    nm, np_ = lax.rem(n + nlon - 1, nlon), lax.rem(n + 1, nlon)

    bar = pltpu.get_barrier_semaphore()

    def greet_lon(r, carry):
        pl.semaphore_signal(bar, inc=1, device_id=(l, lax.rem(n + r, nlon)), device_id_type=MESH)
        return carry

    def greet_lat(r, carry):
        pl.semaphore_signal(bar, inc=1, device_id=(lax.rem(l + r, nlat), n), device_id_type=MESH)
        return carry

    lax.fori_loop(1, nlon, greet_lon, 0)
    lax.fori_loop(1, nlat, greet_lat, 0)
    for a in (lm, lp):
        for c in (nm, np_):
            pl.semaphore_signal(bar, inc=1, device_id=(a, c), device_id_type=MESH)
    pl.semaphore_wait(bar, nlon - 1 + nlat - 1 + 4)

    local = pltpu.make_async_copy(ens, ext.at[pl.ds(2, CLAT), pl.ds(2, CLON)], loc)
    local.start()

    groups = ((0, 1), (1, 2))

    def send1(g):
        b0, nb = groups[g]

        def go(r, carry):
            peer = lax.rem(n + r, nlon)
            pltpu.make_async_remote_copy(
                src_ref=picked.at[pl.ds(b0, nb), pl.ds(peer * piece, piece)],
                dst_ref=got1.at[r - 1, pl.ds(b0, nb)],
                send_sem=s1.at[g],
                recv_sem=r1.at[g],
                device_id=(l, peer),
                device_id_type=MESH,
            ).start()
            return carry

        lax.fori_loop(1, nlon, go, 0)

    def wait1(g):
        b0, nb = groups[g]
        full = got1.at[:, pl.ds(b0, nb)]
        pltpu.make_async_copy(full, full, r1.at[g]).wait()

    def send2(g):
        b0, nb = groups[g]
        tot = picked[pl.ds(b0, nb), pl.ds(pl.multiple_of(n * piece, piece), piece), :]
        for i in range(nlon - 1):
            tot = tot + got1[i, pl.ds(b0, nb)]
        part1[pl.ds(b0, nb)] = tot

        def go(r, carry):
            peer = lax.rem(l + r, nlat)
            pltpu.make_async_remote_copy(
                src_ref=part1.at[pl.ds(b0, nb)],
                dst_ref=got2.at[r - 1, pl.ds(b0, nb)],
                send_sem=s2.at[g],
                recv_sem=r2.at[g],
                device_id=(peer, n),
                device_id_type=MESH,
            ).start()
            return carry

        lax.fori_loop(1, nlat, go, 0)

    def wait2(g):
        b0, nb = groups[g]
        full = got2.at[:, pl.ds(b0, nb)]
        pltpu.make_async_copy(full, full, r2.at[g]).wait()

    def send3(g):
        b0, nb = groups[g]
        tot = part1[pl.ds(b0, nb)]
        for i in range(nlat - 1):
            tot = tot + got2[i, pl.ds(b0, nb)]
        part2[pl.ds(b0, nb)] = tot
        mine = pl.ds(pl.multiple_of(n * piece, piece), piece)
        rows[pl.ds(b0, nb), mine, :] = tot

        def go(r, carry):
            peer = lax.rem(n + r, nlon)
            pltpu.make_async_remote_copy(
                src_ref=part2.at[pl.ds(b0, nb)],
                dst_ref=rows.at[pl.ds(b0, nb), mine],
                send_sem=s3.at[g],
                recv_sem=r3.at[g],
                device_id=(l, peer),
                device_id_type=MESH,
            ).start()
            return carry

        lax.fori_loop(1, nlon, go, 0)

    def wait3(g):
        b0, nb = groups[g]
        full = rows.at[pl.ds(b0, nb), pl.ds(0, NOBS - piece)]
        pltpu.make_async_copy(full, full, r3.at[g]).wait()

    send1(0)
    send1(1)
    wait1(0)
    send2(0)
    wait2(0)
    send3(0)
    wait1(1)
    send2(1)
    wait2(1)
    send3(1)

    moves = (
        ((lm, n), (0, 2, 0, CLON), (34, 2)),
        ((lp, n), (CLAT - 2, 2, 0, CLON), (0, 2)),
        ((l, nm), (0, CLAT, 0, 2), (2, 18)),
        ((l, np_), (0, CLAT, CLON - 2, 2), (2, 0)),
        ((lm, nm), (0, 1, 0, 1), (34, 18)),
        ((lm, np_), (0, 1, CLON - 1, 1), (34, 1)),
        ((lp, nm), (CLAT - 1, 1, 0, 1), (1, 18)),
        ((lp, np_), (CLAT - 1, 1, CLON - 1, 1), (1, 1)),
    )
    copies = []
    for i, (dev, (i0, ni, j0, nj), (di, dj)) in enumerate(moves):
        copies.append(
            pltpu.make_async_remote_copy(
                src_ref=ens.at[pl.ds(i0, ni), pl.ds(j0, nj)],
                dst_ref=ext.at[pl.ds(di, ni), pl.ds(dj, nj)],
                send_sem=hs.at[i],
                recv_sem=hr.at[i],
                device_id=dev,
                device_id_type=MESH,
            )
        )
        if i < 4:
            copies.append(
                pltpu.make_async_remote_copy(
                    src_ref=edges.at[i],
                    dst_ref=edges_in.at[i],
                    send_sem=es.at[i],
                    recv_sem=er.at[i],
                    device_id=dev,
                    device_id_type=MESH,
                )
            )
    for c in copies:
        c.start()
    wait3(0)
    wait3(1)
    for g in range(2):
        b0, nb = groups[g]
        src = picked.at[pl.ds(b0, nb), pl.ds(0, NOBS - piece)]
        pltpu.make_async_copy(src, src, s1.at[g]).wait()
        full = got2.at[:, pl.ds(b0, nb)]
        pltpu.make_async_copy(full, full, s2.at[g]).wait()
        pltpu.make_async_copy(src, src, s3.at[g]).wait()
    for c in copies:
        c.wait()
    local.wait()


def ssum(xs):
    xs = list(xs)
    while len(xs) > 1:
        xs = [xs[i] + xs[i + 1] if i + 1 < len(xs) else xs[i] for i in range(0, len(xs), 2)]
    return xs[0]


def inv_sym(p, b):
    if b == 1:
        return {(0, 0): 1.0 / p[0, 0]}
    if b == 2:
        a, c, d = p[0, 0], p[0, 1], p[1, 1]
        r = 1.0 / (a * d - c * c)
        off = -(c * r)
        return {(0, 0): d * r, (0, 1): off, (1, 0): off, (1, 1): a * r}
    h = b // 2
    hs = range(h)
    A = inv_sym({(s, t): p[s, t] for s in hs for t in range(s, h)}, h)
    B = {(s, t): p[s, h + t] for s in hs for t in hs}
    AB = {(s, t): ssum(A[s, u] * B[u, t] for u in hs) for s in hs for t in hs}
    S = {
        (s, t): p[h + s, h + t] - ssum(B[u, s] * AB[u, t] for u in hs)
        for s in hs
        for t in range(s, h)
    }
    Si = inv_sym(S, h)
    ABS = {(s, t): ssum(AB[s, u] * Si[u, t] for u in hs) for s in hs for t in hs}
    Q = {}
    for s in hs:
        for t in hs:
            Q[s, t] = A[s, t] + ssum(ABS[s, u] * AB[t, u] for u in hs)
            Q[s, h + t] = -ABS[s, t]
            Q[h + t, s] = Q[s, h + t]
            Q[h + s, h + t] = Si[s, t]
    return Q


def sweep_slab(tiles, base, b, nrow):
    rt_n, lt_n = nrow // 8, len(tiles[0])
    lane = lax.broadcasted_iota(jnp.int32, (8, 128), 1)
    sub = lax.broadcasted_iota(jnp.int32, (8, 128), 0)
    tiles = [list(r) for r in tiles]
    full = (8, 128)
    for c in range(0, nrow, b):
        ltc, l0 = (base + c) // 128, (base + c) % 128
        rt0, s0 = c // 8, c % 8
        rows = [
            [jnp.broadcast_to(tiles[rt0][lt][s0 + s : s0 + s + 1, :], full) for lt in range(lt_n)]
            for s in range(b)
        ]
        cols = [
            [
                jnp.broadcast_to(tiles[rt][ltc][:, l0 + s : l0 + s + 1], full)
                for rt in range(rt_n)
            ]
            for s in range(b)
        ]
        p = {
            (s, t): jnp.broadcast_to(rows[s][ltc][:, l0 + t : l0 + t + 1], full)
            for s in range(b)
            for t in range(s, b)
        }
        Q = inv_sym(p, b)
        colm = jnp.logical_and(lane >= l0, lane < l0 + b)
        R = []
        for s in range(b):
            rr = []
            for lt in range(lt_n):
                acc = ssum(Q[s, t] * rows[t][lt] for t in range(b))
                if lt == ltc:
                    for t in range(b):
                        acc = jnp.where(lane == l0 + t, -Q[s, t], acc)
                rr.append(acc)
            R.append(rr)
        for rt in range(rt_n):
            for lt in range(lt_n):
                m = tiles[rt][lt]
                if lt == ltc:
                    m = jnp.where(colm, 0.0, m)
                m = m - ssum(cols[s][rt] * R[s][lt] for s in range(b))
                if rt == rt0:
                    for s in range(b):
                        m = jnp.where(sub == s0 + s, R[s][lt], m)
                tiles[rt][lt] = m
    return tiles


def split3(x):
    h = x.astype(BF16)
    r = x - h.astype(F32)
    m = r.astype(BF16)
    return h, m, (r - m.astype(F32)).astype(BF16)


def split2(x):
    h = x.astype(BF16)
    return h, (x - h.astype(F32)).astype(BF16)


def eliminate(m_ref):
    nb = PANEL
    lane = lax.broadcasted_iota(jnp.int32, (nb, 256), 1)
    cm = lax.broadcasted_iota(jnp.int32, (1, 128), 1)
    count = 256 // nb
    for k in range(count):
        r0 = k * nb
        slab = m_ref[r0 : r0 + nb, 0:256]
        tiles = [
            [m_ref[r0 + 8 * rt : r0 + 8 * rt + 8, 128 * lt : 128 * lt + 128] for lt in range(4)]
            for rt in range(nb // 8)
        ]
        tiles = sweep_slab(tiles, r0, PIV, nb)
        R = jnp.concatenate([jnp.concatenate(t, axis=1) for t in tiles], axis=0)
        left = jnp.where(jnp.logical_and(lane >= r0, lane < r0 + nb), 0.0, slab)
        lh, lm, ll = split3(left)
        rh, rm, rl = split3(R)
        la = jnp.concatenate([lh, lh, lm, lh, lm, ll], axis=0)
        ra = jnp.concatenate([rh, rm, rh, rl, rm, rh], axis=0)
        l0 = (r0 // 128) * 128
        here = jnp.logical_and(cm >= r0 - l0, cm < r0 - l0 + nb)

        def apply(a, z):
            u = lax.dot_general(la[:, a:z], ra, TN, preferred_element_type=F32)
            for lt in range(4):
                cur = m_ref[a:z, 128 * lt : 128 * lt + 128]
                if 128 * lt == l0:
                    cur = jnp.where(here, 0.0, cur)
                m_ref[a:z, 128 * lt : 128 * lt + 128] = cur - u[:, 128 * lt : 128 * lt + 128]

        if k + 1 < count:
            apply(r0 + nb, r0 + 2 * nb)
            if r0 > 0:
                apply(0, r0)
            if r0 + 2 * nb < 256:
                apply(r0 + 2 * nb, 256)
        else:
            apply(0, r0)
        m_ref[r0 : r0 + nb, :] = R


def main_kernel(
    nlat,
    nlon,
    place,
    tiles_ref,
    radius_ref,
    rows_in,
    noise_ref,
    values_ref,
    var_ref,
    cells_ref,
    alat,
    alon,
    diff,
    edge_ref,
    ext,
    out,
    rows_ref,
    x_ref,
    mid_ref,
    o_ref,
    cb_ref,
    m_ref,
    sth_ref,
    stl_ref,
    wh_ref,
    wm_ref,
    wl_ref,
    u_ref,
    v_ref,
    insem,
    outsem,
):
    l = place[0]
    n = place[1]
    load = pltpu.make_async_copy(ext, x_ref, insem)
    load.start()
    for b in range(NB):
        rows_ref[b] = rows_in[b]

    def derived(a, e, k):
        return (
            1.0 - jnp.abs(a) - jnp.abs(e) - 4.0 * k,
            jnp.maximum(a, 0.0) + k,
            k - jnp.minimum(a, 0.0),
            jnp.maximum(e, 0.0) + k,
            k - jnp.minimum(e, 0.0),
        )

    def inner(q, carry):
        i0 = q * 8
        cells = [
            jnp.transpose(r[pl.ds(i0, 8)].reshape(128, LEV)) for r in (alat, alon, diff)
        ]
        for f, d in enumerate(derived(*cells)):
            for i in range(8):
                for j in range(CLON):
                    t = i * CLON + j
                    cb_ref[f, i0 + 1 + i, 1 + j] = jnp.broadcast_to(d[:, t : t + 1], (8, 128))
        return carry

    lax.fori_loop(0, CLAT // 8, inner, 0)
    for d in range(4):
        der = derived(edge_ref[d, 0], edge_ref[d, 1], edge_ref[d, 2])
        if d < 2:
            outside = (l == nlat - 1) if d == 0 else (l == 0)
            keep = jnp.where(outside, 0.0, 1.0)
        for f in range(5):
            w = der[f] * keep if d < 2 else der[f]
            for t in range(CLON if d < 2 else CLAT):
                spread = jnp.broadcast_to(w[:, t : t + 1], (8, 128))
                if d == 0:
                    cb_ref[f, CLAT + 1, 1 + t] = spread
                elif d == 1:
                    cb_ref[f, 0, 1 + t] = spread
                elif d == 2:
                    cb_ref[f, 1 + t, CLON + 1] = spread
                else:
                    cb_ref[f, 1 + t, 0] = spread

    ri = lax.broadcasted_iota(jnp.int32, (256, 256), 0)
    ci = lax.broadcasted_iota(jnp.int32, (256, 256), 1)
    eye = ri == ci
    total_lon = float(CLON * nlon)

    def column(row):
        return jnp.sum(jnp.where(eye, row, 0.0), axis=1, keepdims=True)

    def where_obs(b):
        pos = lax.shift_right_logical(cells_ref[pl.ds(b, 1), :], 3)
        lat = tiles_ref[b, 0] * CLAT + lax.shift_right_logical(pos, 4)
        lon = tiles_ref[b, 1] * CLON + jnp.bitwise_and(pos, 15)
        return lat.astype(F32), lon.astype(F32)

    def lon_sq(gap):
        gap = jnp.abs(gap)
        gap = jnp.minimum(gap, total_lon - gap)
        return gap * gap

    load.wait()

    def batch(b, carry):
        rows = rows_ref[b]
        spread = rows - jnp.mean(rows, axis=1, keepdims=True)
        var = var_ref[pl.ds(b, 1), :]
        cov = lax.dot_general(spread, spread, NT, precision=HI, preferred_element_type=F32)
        m_ref[:, 0:256] = cov * (1.0 / (MEM - 1)) + jnp.where(eye, var, 0.0)
        m_ref[:, 256:512] = (
            column(values_ref[pl.ds(b, 1), :])
            + column(jnp.sqrt(var)) * noise_ref[b]
            - rows
        )
        spread_t = jnp.transpose(spread) * (1.0 / (MEM - 1))
        hi, lo = split2(spread_t)
        sth_ref[...] = hi
        stl_ref[...] = lo
        eliminate(m_ref)
        weights = m_ref[:, 256:512]
        wh_ref[...], wm_ref[...], wl_ref[...] = split3(weights)

        reach = radius_ref[b].astype(F32)
        inv_sq = 1.0 / (jnp.full((1, 256), 1.0, F32) * (reach * reach))
        obs_lat, obs_lon = where_obs(b)

        def later(c, carry):
            r = rows_ref[c]
            mine_lat, mine_lon = where_obs(c)
            dlat = column(mine_lat) - obs_lat
            d2 = dlat * dlat + lon_sq(column(mine_lon) - obs_lon)
            taper = jnp.maximum(1.0 - d2 * inv_sq, 0.0)
            an = r - jnp.mean(r, axis=1, keepdims=True)
            reg = lax.dot_general(an, spread_t, NN, precision=HI, preferred_element_type=F32)
            reg = reg * (taper * taper)
            rows_ref[c] = r + lax.dot_general(
                reg, weights, NN, precision=HI, preferred_element_type=F32
            )
            return carry

        lax.fori_loop(b + 1, NB, later, 0)

        for j in range(CLON + 4):
            pos = lax.rem(n * CLON + j - 2 + CLON * nlon, CLON * nlon).astype(F32)
            v_ref[j] = jnp.broadcast_to(lon_sq(pos - obs_lon) * inv_sq, (8, 256))

        def lat_row(i, carry):
            gap = (l * CLAT + i - 2).astype(F32) - obs_lat
            u_ref[i] = jnp.broadcast_to(1.0 - gap * gap * inv_sq, (8, 256))
            return carry

        lax.fori_loop(0, CLAT + 4, lat_row, 0)

        def block(i, carry):
            x = x_ref[pl.ds(4 * i, 4)].reshape(4 * 20 * 8, 256)
            an = x - jnp.mean(x, axis=1, keepdims=True)
            ah, al = split2(an)
            sh, sl = sth_ref[...], stl_ref[...]
            dot = functools.partial(lax.dot_general, dimension_numbers=NN, preferred_element_type=F32)
            reg = dot(ah, sh) + dot(al, sh) + dot(ah, sl)
            tap = jnp.maximum(u_ref[pl.ds(4 * i, 4)][:, None] - v_ref[...][None], 0.0)
            reg = reg * (tap * tap).reshape(4 * 20 * 8, 256)
            gh, gm, gl = split3(reg)
            wh, wm, wl = wh_ref[...], wm_ref[...], wl_ref[...]
            small = dot(gm, wm) + dot(gh, wl) + dot(gl, wh)
            x = x + (dot(gh, wh) + ((dot(gm, wh) + dot(gh, wm)) + small))
            x_ref[pl.ds(4 * i, 4)] = x.reshape(4, 20, 8, 256)
            return carry

        lax.fori_loop(0, 9, block, 0)
        return carry

    lax.fori_loop(0, NB, batch, 0)

    @pl.when(l == 0)
    def _():
        x_ref[0:2] = jnp.zeros((2, CLON + 4, LEV, MEM), F32)

    @pl.when(l == nlat - 1)
    def _():
        x_ref[CLAT + 2 : CLAT + 4] = jnp.zeros((2, CLON + 4, LEV, MEM), F32)

    def first(i, carry):
        for h in range(2):
            m = pl.ds(128 * h, 128)
            mid_ref[i, :, :, m] = (
                cb_ref[0, i] * x_ref[i + 1, 1:19, :, m]
                + cb_ref[1, i] * x_ref[i, 1:19, :, m]
                + cb_ref[2, i] * x_ref[i + 2, 1:19, :, m]
                + cb_ref[3, i] * x_ref[i + 1, 0:18, :, m]
                + cb_ref[4, i] * x_ref[i + 1, 2:20, :, m]
            )
        return carry

    lax.fori_loop(0, CLAT + 2, first, 0)

    def second(i, carry):
        for h in range(2):
            m = pl.ds(128 * h, 128)
            o_ref[i, :, :, m] = (
                cb_ref[0, i + 1, 1:17] * mid_ref[i + 1, 1:17, :, m]
                + cb_ref[1, i + 1, 1:17] * mid_ref[i, 1:17, :, m]
                + cb_ref[2, i + 1, 1:17] * mid_ref[i + 2, 1:17, :, m]
                + cb_ref[3, i + 1, 1:17] * mid_ref[i + 1, 0:16, :, m]
                + cb_ref[4, i + 1, 1:17] * mid_ref[i + 1, 2:18, :, m]
            )
        pltpu.make_async_copy(o_ref.at[i], out.at[i], outsem).start()
        return carry

    lax.fori_loop(0, CLAT, second, 0)
    pltpu.make_async_copy(o_ref, out, outsem).wait()


def shards(
    nlat,
    nlon,
    ensemble,
    obs_values,
    obs_noise,
    obs_var,
    obs_cells,
    owner_tiles,
    radius,
    courant_lat,
    courant_lon,
    diffusivity,
):
    l = lax.axis_index("lat")
    n = lax.axis_index("lon")
    own = jnp.logical_and(owner_tiles[:, 0] == l, owner_tiles[:, 1] == n).astype(F32)
    place = jnp.stack([l, n]).astype(jnp.int32)

    picked = pl.pallas_call(
        pick_kernel,
        out_shape=jax.ShapeDtypeStruct((NB, NOBS, MEM), F32),
        in_specs=[
            pl.BlockSpec(memory_space=SM),
            pl.BlockSpec(memory_space=SM),
            pl.BlockSpec(memory_space=VM),
        ],
        out_specs=pl.BlockSpec(memory_space=VM),
        compiler_params=pltpu.CompilerParams(vmem_limit_bytes=24 << 20),
        name="pick",
    )(obs_cells, own, ensemble.reshape(-1, MEM))

    coefs = jnp.stack([courant_lat, courant_lon, diffusivity])
    pad = lambda x: jnp.pad(x, ((0, 0), (0, 0), (0, 32 - x.shape[2])))
    edges = jnp.stack(
        [
            pad(jnp.swapaxes(coefs[:, 0], 1, 2)),
            pad(jnp.swapaxes(coefs[:, CLAT - 1], 1, 2)),
            jnp.swapaxes(coefs[:, :, 0], 1, 2),
            jnp.swapaxes(coefs[:, :, CLON - 1], 1, 2),
        ]
    )
    piece = NOBS // nlon
    dma = pltpu.SemaphoreType.DMA
    rows, edges_in, ext = pl.pallas_call(
        functools.partial(exchange_kernel, nlat, nlon),
        out_shape=(
            jax.ShapeDtypeStruct((NB, NOBS, MEM), F32),
            jax.ShapeDtypeStruct((4, 3, LEV, 32), F32),
            jax.ShapeDtypeStruct((CLAT + 4, CLON + 4, LEV, MEM), F32),
        ),
        in_specs=[
            pl.BlockSpec(memory_space=VM),
            pl.BlockSpec(memory_space=VM),
            pl.BlockSpec(memory_space=pl.ANY),
        ],
        out_specs=(
            pl.BlockSpec(memory_space=VM),
            pl.BlockSpec(memory_space=VM),
            pl.BlockSpec(memory_space=pl.ANY),
        ),
        scratch_shapes=[
            pltpu.VMEM((nlon - 1, NB, piece, MEM), F32),
            pltpu.VMEM((nlat - 1, NB, piece, MEM), F32),
            pltpu.VMEM((NB, piece, MEM), F32),
            pltpu.VMEM((NB, piece, MEM), F32),
            dma((2,)),
            dma((2,)),
            dma((2,)),
            dma((2,)),
            dma((2,)),
            dma((2,)),
            dma((8,)),
            dma((8,)),
            dma((4,)),
            dma((4,)),
            dma,
        ],
        compiler_params=pltpu.CompilerParams(
            collective_id=0, has_side_effects=True, vmem_limit_bytes=56 << 20
        ),
        name="exchange",
    )(picked, edges, ensemble)

    return pl.pallas_call(
        functools.partial(main_kernel, nlat, nlon),
        out_shape=jax.ShapeDtypeStruct((CLAT, CLON, LEV, MEM), F32),
        in_specs=[pl.BlockSpec(memory_space=SM)] * 3
        + [pl.BlockSpec(memory_space=VM)] * 9
        + [pl.BlockSpec(memory_space=pl.ANY)],
        out_specs=pl.BlockSpec(memory_space=pl.ANY),
        scratch_shapes=[
            pltpu.VMEM((NB, NOBS, MEM), F32),
            pltpu.VMEM((CLAT + 4, CLON + 4, LEV, MEM), F32),
            pltpu.VMEM((CLAT + 2, CLON + 2, LEV, MEM), F32),
            pltpu.VMEM((CLAT, CLON, LEV, MEM), F32),
            pltpu.VMEM((5, CLAT + 2, CLON + 2, LEV, 128), F32),
            pltpu.VMEM((256, 512), F32),
            pltpu.VMEM((256, 256), BF16),
            pltpu.VMEM((256, 256), BF16),
            pltpu.VMEM((256, 256), BF16),
            pltpu.VMEM((256, 256), BF16),
            pltpu.VMEM((256, 256), BF16),
            pltpu.VMEM((CLAT + 4, LEV, 256), F32),
            pltpu.VMEM((CLON + 4, LEV, 256), F32),
            dma,
            dma,
        ],
        compiler_params=pltpu.CompilerParams(vmem_limit_bytes=56 << 20),
        name="assimilate",
    )(
        place,
        owner_tiles,
        radius,
        rows,
        obs_noise,
        obs_values,
        obs_var,
        obs_cells,
        courant_lat,
        courant_lon,
        diffusivity,
        edges_in,
        ext,
    )


def solution(mesh):
    nlat, nlon = mesh.shape["lat"], mesh.shape["lon"]
    tile = P("lat", "lon", None)
    return jax.shard_map(
        functools.partial(shards, nlat, nlon),
        mesh=mesh,
        in_specs=(P("lat", "lon", None, None),) + (P(),) * 6 + (tile,) * 3,
        out_specs=P("lat", "lon", None, None),
        check_vma=False,
    )
```

```python
import functools

import jax
import jax.numpy as jnp
from jax import lax
from jax.experimental import pallas as pl
from jax.experimental.pallas import tpu as pltpu
from jax.sharding import PartitionSpec as P

F32 = jnp.float32
BF16 = jnp.bfloat16
HI = lax.Precision.HIGHEST
MESH = pl.DeviceIdType.MESH
NN = (((1,), (0,)), ((), ()))
NT = (((1,), (1,)), ((), ()))
TN = (((0,), (0,)), ((), ()))

LEV = 8
NB = 3
CLAT = 32
CLON = 16
NOBS = 256
MEM = 256
PIV = 4
PANEL = 32
VM = pltpu.VMEM
SM = pltpu.SMEM


def exchange_kernel(
    nlat,
    nlon,
    tiles_ref,
    cells_ref,
    ens,
    alat,
    alon,
    diff,
    rows,
    edges_in,
    place,
    ext,
    state,
    picked,
    edges,
    got1,
    got2,
    part1,
    part2,
    s1,
    r1,
    s2,
    r2,
    s3,
    r3,
    hs,
    hr,
    es,
    er,
    loc,
):
    l = lax.axis_index("lat")
    n = lax.axis_index("lon")
    piece = NOBS // nlon
    lm, lp = lax.rem(l + nlat - 1, nlat), lax.rem(l + 1, nlat)
    nm, np_ = lax.rem(n + nlon - 1, nlon), lax.rem(n + 1, nlon)

    load = pltpu.make_async_copy(ens, state, loc)
    load.start()
    bar = pltpu.get_barrier_semaphore()

    def greet_lon(r, carry):
        pl.semaphore_signal(bar, inc=1, device_id=(l, lax.rem(n + r, nlon)), device_id_type=MESH)
        return carry

    def greet_lat(r, carry):
        pl.semaphore_signal(bar, inc=1, device_id=(lax.rem(l + r, nlat), n), device_id_type=MESH)
        return carry

    lax.fori_loop(1, nlon, greet_lon, 0)
    lax.fori_loop(1, nlat, greet_lat, 0)
    for a in (lm, lp):
        for c in (nm, np_):
            pl.semaphore_signal(bar, inc=1, device_id=(a, c), device_id_type=MESH)
    pl.semaphore_wait(bar, nlon - 1 + nlat - 1 + 4)

    place[0] = l
    place[1] = n
    lane = lax.broadcasted_iota(jnp.int32, (LEV, 32), 1)
    for q, coef in enumerate((alat, alon, diff)):
        edges[2, q] = coef[0]
        edges[3, q] = coef[CLON - 1]
        for d, t in ((0, 0), (1, CLAT - 1)):
            line = jnp.zeros((LEV, 32), F32)
            for j in range(CLON):
                line = jnp.where(lane == j, coef[j, :, t : t + 1], line)
            edges[d, q] = line
    flat = state.reshape(CLAT * CLON * LEV, MEM)

    def pick(b):
        own = jnp.logical_and(tiles_ref[0, b] == l, tiles_ref[1, b] == n).astype(F32)

        def body(o, carry):
            for u in range(8):
                c = cells_ref[b, o * 8 + u]
                picked[b, pl.ds(o * 8 + u, 1), :] = flat[pl.ds(c, 1), :] * own
            return carry

        lax.fori_loop(0, NOBS // 8, body, 0)

    load.wait()

    groups = ((0, 1), (1, 2))

    def send1(g):
        b0, nb = groups[g]

        def go(r, carry):
            peer = lax.rem(n + r, nlon)
            pltpu.make_async_remote_copy(
                src_ref=picked.at[pl.ds(b0, nb), pl.ds(peer * piece, piece)],
                dst_ref=got1.at[r - 1, pl.ds(b0, nb)],
                send_sem=s1.at[g],
                recv_sem=r1.at[g],
                device_id=(l, peer),
                device_id_type=MESH,
            ).start()
            return carry

        lax.fori_loop(1, nlon, go, 0)

    def wait1(g):
        b0, nb = groups[g]
        full = got1.at[:, pl.ds(b0, nb)]
        pltpu.make_async_copy(full, full, r1.at[g]).wait()

    def send2(g):
        b0, nb = groups[g]
        tot = picked[pl.ds(b0, nb), pl.ds(pl.multiple_of(n * piece, piece), piece), :]
        for i in range(nlon - 1):
            tot = tot + got1[i, pl.ds(b0, nb)]
        part1[pl.ds(b0, nb)] = tot

        def go(r, carry):
            peer = lax.rem(l + r, nlat)
            pltpu.make_async_remote_copy(
                src_ref=part1.at[pl.ds(b0, nb)],
                dst_ref=got2.at[r - 1, pl.ds(b0, nb)],
                send_sem=s2.at[g],
                recv_sem=r2.at[g],
                device_id=(peer, n),
                device_id_type=MESH,
            ).start()
            return carry

        lax.fori_loop(1, nlat, go, 0)

    def wait2(g):
        b0, nb = groups[g]
        full = got2.at[:, pl.ds(b0, nb)]
        pltpu.make_async_copy(full, full, r2.at[g]).wait()

    def send3(g):
        b0, nb = groups[g]
        tot = part1[pl.ds(b0, nb)]
        for i in range(nlat - 1):
            tot = tot + got2[i, pl.ds(b0, nb)]
        part2[pl.ds(b0, nb)] = tot
        mine = pl.ds(pl.multiple_of(n * piece, piece), piece)
        rows[pl.ds(b0, nb), mine, :] = tot

        def go(r, carry):
            peer = lax.rem(n + r, nlon)
            pltpu.make_async_remote_copy(
                src_ref=part2.at[pl.ds(b0, nb)],
                dst_ref=rows.at[pl.ds(b0, nb), mine],
                send_sem=s3.at[g],
                recv_sem=r3.at[g],
                device_id=(l, peer),
                device_id_type=MESH,
            ).start()
            return carry

        lax.fori_loop(1, nlon, go, 0)

    def wait3(g):
        b0, nb = groups[g]
        full = rows.at[pl.ds(b0, nb), pl.ds(0, NOBS - piece)]
        pltpu.make_async_copy(full, full, r3.at[g]).wait()

    pick(0)
    send1(0)
    pick(1)
    pick(2)
    send1(1)
    wait1(0)
    send2(0)
    wait2(0)
    send3(0)
    wait1(1)
    send2(1)
    wait2(1)
    send3(1)

    moves = (
        ((lm, n), (0, 2, 0, CLON), (34, 2)),
        ((lp, n), (CLAT - 2, 2, 0, CLON), (0, 2)),
        ((l, nm), (0, CLAT, 0, 2), (2, 18)),
        ((l, np_), (0, CLAT, CLON - 2, 2), (2, 0)),
        ((lm, nm), (0, 1, 0, 1), (34, 18)),
        ((lm, np_), (0, 1, CLON - 1, 1), (34, 1)),
        ((lp, nm), (CLAT - 1, 1, 0, 1), (1, 18)),
        ((lp, np_), (CLAT - 1, 1, CLON - 1, 1), (1, 1)),
    )
    copies = []
    for i, (dev, (i0, ni, j0, nj), (di, dj)) in enumerate(moves):
        copies.append(
            pltpu.make_async_remote_copy(
                src_ref=ens.at[pl.ds(i0, ni), pl.ds(j0, nj)],
                dst_ref=ext.at[pl.ds(di, ni), pl.ds(dj, nj)],
                send_sem=hs.at[i],
                recv_sem=hr.at[i],
                device_id=dev,
                device_id_type=MESH,
            )
        )
        if i < 4:
            copies.append(
                pltpu.make_async_remote_copy(
                    src_ref=edges.at[i],
                    dst_ref=edges_in.at[i],
                    send_sem=es.at[i],
                    recv_sem=er.at[i],
                    device_id=dev,
                    device_id_type=MESH,
                )
            )
    for c in copies:
        c.start()
    wait3(0)
    wait3(1)
    for g in range(2):
        b0, nb = groups[g]
        src = picked.at[pl.ds(b0, nb), pl.ds(0, NOBS - piece)]
        pltpu.make_async_copy(src, src, s1.at[g]).wait()
        full = got2.at[:, pl.ds(b0, nb)]
        pltpu.make_async_copy(full, full, s2.at[g]).wait()
        pltpu.make_async_copy(src, src, s3.at[g]).wait()
    for c in copies:
        c.wait()


def ssum(xs):
    xs = list(xs)
    while len(xs) > 1:
        xs = [xs[i] + xs[i + 1] if i + 1 < len(xs) else xs[i] for i in range(0, len(xs), 2)]
    return xs[0]


def inv_sym(p, b):
    if b == 1:
        return {(0, 0): 1.0 / p[0, 0]}
    if b == 2:
        a, c, d = p[0, 0], p[0, 1], p[1, 1]
        r = 1.0 / (a * d - c * c)
        off = -(c * r)
        return {(0, 0): d * r, (0, 1): off, (1, 0): off, (1, 1): a * r}
    h = b // 2
    hs = range(h)
    A = inv_sym({(s, t): p[s, t] for s in hs for t in range(s, h)}, h)
    B = {(s, t): p[s, h + t] for s in hs for t in hs}
    AB = {(s, t): ssum(A[s, u] * B[u, t] for u in hs) for s in hs for t in hs}
    S = {
        (s, t): p[h + s, h + t] - ssum(B[u, s] * AB[u, t] for u in hs)
        for s in hs
        for t in range(s, h)
    }
    Si = inv_sym(S, h)
    ABS = {(s, t): ssum(AB[s, u] * Si[u, t] for u in hs) for s in hs for t in hs}
    Q = {}
    for s in hs:
        for t in hs:
            Q[s, t] = A[s, t] + ssum(ABS[s, u] * AB[t, u] for u in hs)
            Q[s, h + t] = -ABS[s, t]
            Q[h + t, s] = Q[s, h + t]
            Q[h + s, h + t] = Si[s, t]
    return Q


def sweep_slab(tiles, base, b, nrow):
    rt_n, lt_n = nrow // 8, len(tiles[0])
    lane = lax.broadcasted_iota(jnp.int32, (8, 128), 1)
    sub = lax.broadcasted_iota(jnp.int32, (8, 128), 0)
    tiles = [list(r) for r in tiles]
    full = (8, 128)
    for c in range(0, nrow, b):
        ltc, l0 = (base + c) // 128, (base + c) % 128
        rt0, s0 = c // 8, c % 8
        rows = [
            [jnp.broadcast_to(tiles[rt0][lt][s0 + s : s0 + s + 1, :], full) for lt in range(lt_n)]
            for s in range(b)
        ]
        cols = [
            [
                jnp.broadcast_to(tiles[rt][ltc][:, l0 + s : l0 + s + 1], full)
                for rt in range(rt_n)
            ]
            for s in range(b)
        ]
        p = {
            (s, t): jnp.broadcast_to(rows[s][ltc][:, l0 + t : l0 + t + 1], full)
            for s in range(b)
            for t in range(s, b)
        }
        Q = inv_sym(p, b)
        colm = jnp.logical_and(lane >= l0, lane < l0 + b)
        R = []
        for s in range(b):
            rr = []
            for lt in range(lt_n):
                acc = ssum(Q[s, t] * rows[t][lt] for t in range(b))
                if lt == ltc:
                    for t in range(b):
                        acc = jnp.where(lane == l0 + t, -Q[s, t], acc)
                rr.append(acc)
            R.append(rr)
        for rt in range(rt_n):
            for lt in range(lt_n):
                m = tiles[rt][lt]
                if lt == ltc:
                    m = jnp.where(colm, 0.0, m)
                m = m - ssum(cols[s][rt] * R[s][lt] for s in range(b))
                if rt == rt0:
                    for s in range(b):
                        m = jnp.where(sub == s0 + s, R[s][lt], m)
                tiles[rt][lt] = m
    return tiles


def split3(x):
    h = x.astype(BF16)
    r = x - h.astype(F32)
    m = r.astype(BF16)
    return h, m, (r - m.astype(F32)).astype(BF16)


def split2(x):
    h = x.astype(BF16)
    return h, (x - h.astype(F32)).astype(BF16)


def panel(m_ref, k):
    nb = PANEL
    lane = lax.broadcasted_iota(jnp.int32, (nb, 256), 1)
    cm = lax.broadcasted_iota(jnp.int32, (1, 128), 1)
    r0 = k * nb
    slab = m_ref[r0 : r0 + nb, 0:256]
    tiles = [
        [m_ref[r0 + 8 * rt : r0 + 8 * rt + 8, 128 * lt : 128 * lt + 128] for lt in range(4)]
        for rt in range(nb // 8)
    ]
    tiles = sweep_slab(tiles, r0, PIV, nb)
    R = jnp.concatenate([jnp.concatenate(t, axis=1) for t in tiles], axis=0)
    left = jnp.where(jnp.logical_and(lane >= r0, lane < r0 + nb), 0.0, slab)
    lh, lm, ll = split3(left)
    rh, rm, rl = split3(R)
    la = jnp.concatenate([lh, lh, lm, lh, lm, ll], axis=0)
    ra = jnp.concatenate([rh, rm, rh, rl, rm, rh], axis=0)
    l0 = (r0 // 128) * 128
    here = jnp.logical_and(cm >= r0 - l0, cm < r0 - l0 + nb)

    def apply(a, z):
        u = lax.dot_general(la[:, a:z], ra, TN, preferred_element_type=F32)
        for lt in range(4):
            cur = m_ref[a:z, 128 * lt : 128 * lt + 128]
            if 128 * lt == l0:
                cur = jnp.where(here, 0.0, cur)
            m_ref[a:z, 128 * lt : 128 * lt + 128] = cur - u[:, 128 * lt : 128 * lt + 128]

    if r0 + nb < 256:
        apply(r0 + nb, r0 + 2 * nb)
    if r0 > 0:
        apply(0, r0)
    if r0 + 2 * nb < 256:
        apply(r0 + 2 * nb, 256)
    m_ref[r0 : r0 + nb, :] = R


dot = functools.partial(lax.dot_general, dimension_numbers=NN, preferred_element_type=F32)
exact = functools.partial(dot, precision=HI)
GRP = 4


def main_kernel(
    nlat,
    nlon,
    place,
    tiles_ref,
    radius_ref,
    rows_in,
    noise_ref,
    values_ref,
    var_ref,
    cells_ref,
    alat,
    alon,
    diff,
    edge_ref,
    ens,
    ext,
    out,
    rows_ref,
    x_ref,
    reg_ref,
    mid_ref,
    o_ref,
    cb_ref,
    m_ref,
    st_ref,
    sth_ref,
    stl_ref,
    w_ref,
    wh_ref,
    wm_ref,
    wl_ref,
    g_ref,
    u_ref,
    v_ref,
    insem,
    outsem,
):
    l = place[0]
    n = place[1]
    loads = [
        pltpu.make_async_copy(src, x_ref.at[pl.ds(i, ni), pl.ds(j, nj)], insem.at[s])
        for s, (src, i, ni, j, nj) in enumerate(
            (
                (ens, 2, CLAT, 2, CLON),
                (ext.at[pl.ds(0, 2)], 0, 2, 0, CLON + 4),
                (ext.at[pl.ds(CLAT + 2, 2)], CLAT + 2, 2, 0, CLON + 4),
                (ext.at[pl.ds(2, CLAT), pl.ds(0, 2)], 2, CLAT, 0, 2),
                (ext.at[pl.ds(2, CLAT), pl.ds(CLON + 2, 2)], 2, CLAT, CLON + 2, 2),
            )
        )
    ]
    for c in loads:
        c.start()
    for b in range(NB):
        rows_ref[b] = rows_in[b]

    def derived(a, e, k):
        return (
            1.0 - jnp.abs(a) - jnp.abs(e) - 4.0 * k,
            jnp.maximum(a, 0.0) + k,
            k - jnp.minimum(a, 0.0),
            jnp.maximum(e, 0.0) + k,
            k - jnp.minimum(e, 0.0),
        )

    def spread_column(j):
        for f, d in enumerate(derived(alat[j], alon[j], diff[j])):
            for i in range(CLAT):
                cb_ref[f, 1 + i, 1 + j] = jnp.broadcast_to(d[:, i : i + 1], (8, 128))

    def spread_edge(d):
        der = derived(edge_ref[d, 0], edge_ref[d, 1], edge_ref[d, 2])
        if d < 2:
            outside = (l == nlat - 1) if d == 0 else (l == 0)
            keep = jnp.where(outside, 0.0, 1.0)
        for f in range(5):
            w = der[f] * keep if d < 2 else der[f]
            for t in range(CLON if d < 2 else CLAT):
                line = jnp.broadcast_to(w[:, t : t + 1], (8, 128))
                if d == 0:
                    cb_ref[f, CLAT + 1, 1 + t] = line
                elif d == 1:
                    cb_ref[f, 0, 1 + t] = line
                elif d == 2:
                    cb_ref[f, 1 + t, CLON + 1] = line
                else:
                    cb_ref[f, 1 + t, 0] = line

    ri = lax.broadcasted_iota(jnp.int32, (256, 256), 0)
    ci = lax.broadcasted_iota(jnp.int32, (256, 256), 1)
    eye = ri == ci
    total_lon = float(CLON * nlon)

    def column(row):
        return jnp.sum(jnp.where(eye, row, 0.0), axis=1, keepdims=True)

    def where_obs(b):
        pos = lax.shift_right_logical(cells_ref[pl.ds(b, 1), :], 3)
        lat = tiles_ref[0, b] * CLAT + lax.shift_right_logical(pos, 4)
        lon = tiles_ref[1, b] * CLON + jnp.bitwise_and(pos, 15)
        return lat.astype(F32), lon.astype(F32)

    def lon_sq(gap):
        gap = jnp.abs(gap)
        gap = jnp.minimum(gap, total_lon - gap)
        return gap * gap

    def prologue(b):
        rows = rows_ref[b]
        spread = rows - jnp.mean(rows, axis=1, keepdims=True)
        var = var_ref[pl.ds(b, 1), :]
        cov = lax.dot_general(spread, spread, NT, precision=HI, preferred_element_type=F32)
        m_ref[:, 0:256] = cov * (1.0 / (MEM - 1)) + jnp.where(eye, var, 0.0)
        m_ref[:, 256:512] = (
            column(values_ref[pl.ds(b, 1), :])
            + column(jnp.sqrt(var)) * noise_ref[b]
            - rows
        )
        spread_t = jnp.transpose(spread) * (1.0 / (MEM - 1))
        st_ref[...] = spread_t
        sth_ref[...], stl_ref[...] = split2(spread_t)
        reach = radius_ref[b].astype(F32)
        inv_sq = 1.0 / (jnp.full((1, 256), 1.0, F32) * (reach * reach))
        obs_lat, obs_lon = where_obs(b)
        for j in range(CLON + 4):
            pos = lax.rem(n * CLON + j - 2 + CLON * nlon, CLON * nlon).astype(F32)
            v_ref[j] = jnp.broadcast_to(lon_sq(pos - obs_lon) * inv_sq, (8, 256))
        for i in range(CLAT + 4):
            gap = (l * CLAT + i - 2).astype(F32) - obs_lat
            u_ref[i] = jnp.broadcast_to(1.0 - gap * gap * inv_sq, (8, 256))
        return obs_lat, obs_lon, inv_sq

    def regress_rows(c, where):
        obs_lat, obs_lon, inv_sq = where
        r = rows_ref[c]
        mine_lat, mine_lon = where_obs(c)
        dlat = column(mine_lat) - obs_lat
        d2 = dlat * dlat + lon_sq(column(mine_lon) - obs_lon)
        taper = jnp.maximum(1.0 - d2 * inv_sq, 0.0)
        an = r - jnp.mean(r, axis=1, keepdims=True)
        g_ref[c] = exact(an, st_ref[...]) * (taper * taper)

    size = GRP * (CLON + 4) * LEV

    def adjust(i):
        at = pl.ds(GRP * i, GRP)
        x = x_ref[at].reshape(size, MEM)
        gh, gm, gl = split3(reg_ref[at].reshape(size, 256))
        wh, wm, wl = wh_ref[...], wm_ref[...], wl_ref[...]
        small = dot(gm, wm) + dot(gh, wl) + dot(gl, wh)
        x = x + (dot(gh, wh) + ((dot(gm, wh) + dot(gh, wm)) + small))
        x_ref[at] = x.reshape(GRP, CLON + 4, LEV, MEM)
        return x

    def regress(i, x=None):
        at = pl.ds(GRP * i, GRP)
        if x is None:
            x = x_ref[at].reshape(size, MEM)
        ah, al = split2(x - jnp.mean(x, axis=1, keepdims=True))
        sh, sl = sth_ref[...], stl_ref[...]
        reg = dot(ah, sh) + (dot(al, sh) + dot(ah, sl))
        tap = jnp.maximum(u_ref[at][:, None] - v_ref[...][None], 0.0)
        reg = reg * (tap * tap).reshape(size, 256)
        reg_ref[at] = reg.reshape(GRP, CLON + 4, LEV, 256)

    def keep_weights():
        weights = m_ref[:, 256:512]
        w_ref[...] = weights
        wh_ref[...], wm_ref[...], wl_ref[...] = split3(weights)

    where = prologue(0)
    for c in loads:
        c.wait()
    for k in range(8):
        panel(m_ref, k)
        spread_column(2 * k)
        spread_column(2 * k + 1)
        if k < 4:
            spread_edge(k)
        regress(k)
        if k == 7:
            regress(8)
        if k == 3:
            regress_rows(1, where)
        if k == 4:
            regress_rows(2, where)
    keep_weights()

    def batch(b, carry):
        rows_ref[b] = rows_ref[b] + exact(g_ref[b], w_ref[...])
        where = prologue(b)
        for k in range(8):
            panel(m_ref, k)
            regress(k, adjust(k))
            if k == 7:
                regress(8, adjust(8))
            if k == 0:
                rows_ref[2] = rows_ref[2] + exact(g_ref[2], w_ref[...])
            if k == 3:
                regress_rows(2, where)
        keep_weights()
        return carry

    lax.fori_loop(1, NB, batch, 0)

    def last(i, carry):
        adjust(i)
        return carry

    lax.fori_loop(0, 9, last, 0)

    @pl.when(l == 0)
    def _():
        x_ref[0:2] = jnp.zeros((2, CLON + 4, LEV, MEM), F32)

    @pl.when(l == nlat - 1)
    def _():
        x_ref[CLAT + 2 : CLAT + 4] = jnp.zeros((2, CLON + 4, LEV, MEM), F32)

    def first(i, carry):
        for h in range(2):
            m = pl.ds(128 * h, 128)
            mid_ref[i, :, :, m] = (
                cb_ref[0, i] * x_ref[i + 1, 1:19, :, m]
                + cb_ref[1, i] * x_ref[i, 1:19, :, m]
                + cb_ref[2, i] * x_ref[i + 2, 1:19, :, m]
                + cb_ref[3, i] * x_ref[i + 1, 0:18, :, m]
                + cb_ref[4, i] * x_ref[i + 1, 2:20, :, m]
            )
        return carry

    lax.fori_loop(0, CLAT + 2, first, 0)

    def second(i, carry):
        for h in range(2):
            m = pl.ds(128 * h, 128)
            o_ref[i, :, :, m] = (
                cb_ref[0, i + 1, 1:17] * mid_ref[i + 1, 1:17, :, m]
                + cb_ref[1, i + 1, 1:17] * mid_ref[i, 1:17, :, m]
                + cb_ref[2, i + 1, 1:17] * mid_ref[i + 2, 1:17, :, m]
                + cb_ref[3, i + 1, 1:17] * mid_ref[i + 1, 0:16, :, m]
                + cb_ref[4, i + 1, 1:17] * mid_ref[i + 1, 2:18, :, m]
            )
        pltpu.make_async_copy(o_ref.at[i], out.at[i], outsem).start()
        return carry

    lax.fori_loop(0, CLAT, second, 0)
    pltpu.make_async_copy(o_ref, out, outsem).wait()


def main_call(nlat, nlon):
    dma = pltpu.SemaphoreType.DMA
    sq = lambda t: pltpu.VMEM((256, 256), t)
    return pl.pallas_call(
        functools.partial(main_kernel, nlat, nlon),
        out_shape=jax.ShapeDtypeStruct((CLAT, CLON, LEV, MEM), F32),
        in_specs=[pl.BlockSpec(memory_space=SM)] * 3
        + [pl.BlockSpec(memory_space=VM)] * 9
        + [pl.BlockSpec(memory_space=pl.ANY)] * 2,
        out_specs=pl.BlockSpec(memory_space=pl.ANY),
        scratch_shapes=[
            pltpu.VMEM((NB, NOBS, MEM), F32),
            pltpu.VMEM((CLAT + 4, CLON + 4, LEV, MEM), F32),
            pltpu.VMEM((CLAT + 4, CLON + 4, LEV, NOBS), F32),
            pltpu.VMEM((CLAT + 2, CLON + 2, LEV, MEM), F32),
            pltpu.VMEM((CLAT, CLON, LEV, MEM), F32),
            pltpu.VMEM((5, CLAT + 2, CLON + 2, LEV, 128), F32),
            pltpu.VMEM((256, 512), F32),
            sq(F32),
            sq(BF16),
            sq(BF16),
            sq(F32),
            sq(BF16),
            sq(BF16),
            sq(BF16),
            pltpu.VMEM((NB, 256, 256), F32),
            pltpu.VMEM((CLAT + 4, LEV, 256), F32),
            pltpu.VMEM((CLON + 4, LEV, 256), F32),
            dma((5,)),
            dma,
        ],
        compiler_params=pltpu.CompilerParams(vmem_limit_bytes=60 << 20),
        name="assimilate",
    )


def shards(
    nlat,
    nlon,
    ensemble,
    obs_values,
    obs_noise,
    obs_var,
    obs_cells,
    owner_tiles,
    radius,
    courant_lat,
    courant_lon,
    diffusivity,
):
    piece = NOBS // nlon
    dma = pltpu.SemaphoreType.DMA
    tiles = owner_tiles.T
    coefs = [jnp.transpose(c, (1, 2, 0)) for c in (courant_lat, courant_lon, diffusivity)]
    vm = pl.BlockSpec(memory_space=VM)
    sm = pl.BlockSpec(memory_space=SM)
    anym = pl.BlockSpec(memory_space=pl.ANY)
    rows, edges_in, place, ext = pl.pallas_call(
        functools.partial(exchange_kernel, nlat, nlon),
        out_shape=(
            jax.ShapeDtypeStruct((NB, NOBS, MEM), F32),
            jax.ShapeDtypeStruct((4, 3, LEV, 32), F32),
            jax.ShapeDtypeStruct((2,), jnp.int32),
            jax.ShapeDtypeStruct((CLAT + 4, CLON + 4, LEV, MEM), F32),
        ),
        in_specs=[sm, sm, anym, vm, vm, vm],
        out_specs=(vm, vm, sm, anym),
        scratch_shapes=[
            pltpu.VMEM((CLAT, CLON, LEV, MEM), F32),
            pltpu.VMEM((NB, NOBS, MEM), F32),
            pltpu.VMEM((4, 3, LEV, 32), F32),
            pltpu.VMEM((nlon - 1, NB, piece, MEM), F32),
            pltpu.VMEM((nlat - 1, NB, piece, MEM), F32),
            pltpu.VMEM((NB, piece, MEM), F32),
            pltpu.VMEM((NB, piece, MEM), F32),
            dma((2,)),
            dma((2,)),
            dma((2,)),
            dma((2,)),
            dma((2,)),
            dma((2,)),
            dma((8,)),
            dma((8,)),
            dma((4,)),
            dma((4,)),
            dma,
        ],
        compiler_params=pltpu.CompilerParams(
            collective_id=0, has_side_effects=True, vmem_limit_bytes=56 << 20
        ),
        name="exchange",
    )(tiles, obs_cells, ensemble, *coefs)

    return main_call(nlat, nlon)(
        place,
        tiles,
        radius,
        rows,
        obs_noise,
        obs_values,
        obs_var,
        obs_cells,
        *coefs,
        edges_in,
        ensemble,
        ext,
    )


def solution(mesh):
    nlat, nlon = mesh.shape["lat"], mesh.shape["lon"]
    tile = P("lat", "lon", None)
    return jax.shard_map(
        functools.partial(shards, nlat, nlon),
        mesh=mesh,
        in_specs=(P("lat", "lon", None, None),) + (P(),) * 6 + (tile,) * 3,
        out_specs=P("lat", "lon", None, None),
        check_vma=False,
    )
```

```python
import functools

import jax
import jax.numpy as jnp
from jax import lax
from jax.experimental import pallas as pl
from jax.experimental.pallas import tpu as pltpu
from jax.sharding import PartitionSpec as P

F32 = jnp.float32
BF16 = jnp.bfloat16
HI = lax.Precision.HIGHEST
MESH = pl.DeviceIdType.MESH
NN = (((1,), (0,)), ((), ()))
NT = (((1,), (1,)), ((), ()))
TN = (((0,), (0,)), ((), ()))

LEV = 8
NB = 3
CLAT = 32
CLON = 16
NOBS = 256
MEM = 256
PIV = 4
PANEL = 32
VM = pltpu.VMEM
SM = pltpu.SMEM


def exchange_kernel(
    nlat,
    nlon,
    tiles_ref,
    cells_ref,
    ens,
    alat,
    alon,
    diff,
    rows,
    edges_in,
    place,
    ext,
    state,
    picked,
    edges,
    got1,
    got2,
    part1,
    part2,
    s1,
    r1,
    s2,
    r2,
    s3,
    r3,
    hs,
    hr,
    es,
    er,
    loc,
):
    l = lax.axis_index("lat")
    n = lax.axis_index("lon")
    piece = NOBS // nlon
    lm, lp = lax.rem(l + nlat - 1, nlat), lax.rem(l + 1, nlat)
    nm, np_ = lax.rem(n + nlon - 1, nlon), lax.rem(n + 1, nlon)

    load = pltpu.make_async_copy(ens, state, loc)
    load.start()
    bar = pltpu.get_barrier_semaphore()

    def greet_lon(r, carry):
        pl.semaphore_signal(bar, inc=1, device_id=(l, lax.rem(n + r, nlon)), device_id_type=MESH)
        return carry

    def greet_lat(r, carry):
        pl.semaphore_signal(bar, inc=1, device_id=(lax.rem(l + r, nlat), n), device_id_type=MESH)
        return carry

    lax.fori_loop(1, nlon, greet_lon, 0)
    lax.fori_loop(1, nlat, greet_lat, 0)
    for a in (lm, lp):
        for c in (nm, np_):
            pl.semaphore_signal(bar, inc=1, device_id=(a, c), device_id_type=MESH)
    pl.semaphore_wait(bar, nlon - 1 + nlat - 1 + 4)

    place[0] = l
    place[1] = n
    lane = lax.broadcasted_iota(jnp.int32, (LEV, 32), 1)
    for q, coef in enumerate((alat, alon, diff)):
        edges[2, q] = coef[0]
        edges[3, q] = coef[CLON - 1]
        for d, t in ((0, 0), (1, CLAT - 1)):
            line = jnp.zeros((LEV, 32), F32)
            for j in range(CLON):
                line = jnp.where(lane == j, coef[j, :, t : t + 1], line)
            edges[d, q] = line
    flat = state.reshape(CLAT * CLON * LEV, MEM)

    def pick(b):
        own = jnp.logical_and(tiles_ref[0, b] == l, tiles_ref[1, b] == n).astype(F32)

        def body(o, carry):
            for u in range(8):
                c = cells_ref[b, o * 8 + u]
                picked[b, pl.ds(o * 8 + u, 1), :] = flat[pl.ds(c, 1), :] * own
            return carry

        lax.fori_loop(0, NOBS // 8, body, 0)

    load.wait()

    groups = ((0, 1), (1, 2))

    def send1(g):
        b0, nb = groups[g]

        def go(r, carry):
            peer = lax.rem(n + r, nlon)
            pltpu.make_async_remote_copy(
                src_ref=picked.at[pl.ds(b0, nb), pl.ds(peer * piece, piece)],
                dst_ref=got1.at[r - 1, pl.ds(b0, nb)],
                send_sem=s1.at[g],
                recv_sem=r1.at[g],
                device_id=(l, peer),
                device_id_type=MESH,
            ).start()
            return carry

        lax.fori_loop(1, nlon, go, 0)

    def wait1(g):
        b0, nb = groups[g]
        full = got1.at[:, pl.ds(b0, nb)]
        pltpu.make_async_copy(full, full, r1.at[g]).wait()

    def send2(g):
        b0, nb = groups[g]
        tot = picked[pl.ds(b0, nb), pl.ds(pl.multiple_of(n * piece, piece), piece), :]
        for i in range(nlon - 1):
            tot = tot + got1[i, pl.ds(b0, nb)]
        part1[pl.ds(b0, nb)] = tot

        def go(r, carry):
            peer = lax.rem(l + r, nlat)
            pltpu.make_async_remote_copy(
                src_ref=part1.at[pl.ds(b0, nb)],
                dst_ref=got2.at[r - 1, pl.ds(b0, nb)],
                send_sem=s2.at[g],
                recv_sem=r2.at[g],
                device_id=(peer, n),
                device_id_type=MESH,
            ).start()
            return carry

        lax.fori_loop(1, nlat, go, 0)

    def wait2(g):
        b0, nb = groups[g]
        full = got2.at[:, pl.ds(b0, nb)]
        pltpu.make_async_copy(full, full, r2.at[g]).wait()

    def send3(g):
        b0, nb = groups[g]
        tot = part1[pl.ds(b0, nb)]
        for i in range(nlat - 1):
            tot = tot + got2[i, pl.ds(b0, nb)]
        part2[pl.ds(b0, nb)] = tot
        mine = pl.ds(pl.multiple_of(n * piece, piece), piece)
        rows[pl.ds(b0, nb), mine, :] = tot

        def go(r, carry):
            peer = lax.rem(n + r, nlon)
            pltpu.make_async_remote_copy(
                src_ref=part2.at[pl.ds(b0, nb)],
                dst_ref=rows.at[pl.ds(b0, nb), mine],
                send_sem=s3.at[g],
                recv_sem=r3.at[g],
                device_id=(l, peer),
                device_id_type=MESH,
            ).start()
            return carry

        lax.fori_loop(1, nlon, go, 0)

    def wait3(g):
        b0, nb = groups[g]
        full = rows.at[pl.ds(b0, nb), pl.ds(0, NOBS - piece)]
        pltpu.make_async_copy(full, full, r3.at[g]).wait()

    pick(0)
    send1(0)
    pick(1)
    pick(2)
    send1(1)

    moves = (
        ((lm, n), (0, 2, 0, CLON), (34, 2)),
        ((lp, n), (CLAT - 2, 2, 0, CLON), (0, 2)),
        ((l, nm), (0, CLAT, 0, 2), (2, 18)),
        ((l, np_), (0, CLAT, CLON - 2, 2), (2, 0)),
        ((lm, nm), (0, 1, 0, 1), (34, 18)),
        ((lm, np_), (0, 1, CLON - 1, 1), (34, 1)),
        ((lp, nm), (CLAT - 1, 1, 0, 1), (1, 18)),
        ((lp, np_), (CLAT - 1, 1, CLON - 1, 1), (1, 1)),
    )
    copies = []
    for i, (dev, (i0, ni, j0, nj), (di, dj)) in enumerate(moves):
        copies.append(
            pltpu.make_async_remote_copy(
                src_ref=ens.at[pl.ds(i0, ni), pl.ds(j0, nj)],
                dst_ref=ext.at[pl.ds(di, ni), pl.ds(dj, nj)],
                send_sem=hs.at[i],
                recv_sem=hr.at[i],
                device_id=dev,
                device_id_type=MESH,
            )
        )
        if i < 4:
            copies.append(
                pltpu.make_async_remote_copy(
                    src_ref=edges.at[i],
                    dst_ref=edges_in.at[i],
                    send_sem=es.at[i],
                    recv_sem=er.at[i],
                    device_id=dev,
                    device_id_type=MESH,
                )
            )
    for c in copies:
        c.start()

    wait1(0)
    send2(0)
    wait2(0)
    send3(0)
    wait1(1)
    send2(1)
    wait2(1)
    send3(1)

    wait3(0)
    wait3(1)
    for g in range(2):
        b0, nb = groups[g]
        src = picked.at[pl.ds(b0, nb), pl.ds(0, NOBS - piece)]
        pltpu.make_async_copy(src, src, s1.at[g]).wait()
        full = got2.at[:, pl.ds(b0, nb)]
        pltpu.make_async_copy(full, full, s2.at[g]).wait()
        pltpu.make_async_copy(src, src, s3.at[g]).wait()
    for c in copies:
        c.wait()


def ssum(xs):
    xs = list(xs)
    while len(xs) > 1:
        xs = [xs[i] + xs[i + 1] if i + 1 < len(xs) else xs[i] for i in range(0, len(xs), 2)]
    return xs[0]


def inv_sym(p, b):
    if b == 1:
        return {(0, 0): 1.0 / p[0, 0]}
    if b == 2:
        a, c, d = p[0, 0], p[0, 1], p[1, 1]
        r = 1.0 / (a * d - c * c)
        off = -(c * r)
        return {(0, 0): d * r, (0, 1): off, (1, 0): off, (1, 1): a * r}
    h = b // 2
    hs = range(h)
    A = inv_sym({(s, t): p[s, t] for s in hs for t in range(s, h)}, h)
    B = {(s, t): p[s, h + t] for s in hs for t in hs}
    AB = {(s, t): ssum(A[s, u] * B[u, t] for u in hs) for s in hs for t in hs}
    S = {
        (s, t): p[h + s, h + t] - ssum(B[u, s] * AB[u, t] for u in hs)
        for s in hs
        for t in range(s, h)
    }
    Si = inv_sym(S, h)
    ABS = {(s, t): ssum(AB[s, u] * Si[u, t] for u in hs) for s in hs for t in hs}
    Q = {}
    for s in hs:
        for t in hs:
            Q[s, t] = A[s, t] + ssum(ABS[s, u] * AB[t, u] for u in hs)
            Q[s, h + t] = -ABS[s, t]
            Q[h + t, s] = Q[s, h + t]
            Q[h + s, h + t] = Si[s, t]
    return Q


def sweep_slab(tiles, base, b, nrow, scr, hooks=()):
    rt_n, lt_n = nrow // 8, len(tiles[0])
    lane = lax.broadcasted_iota(jnp.int32, (8, 128), 1)
    sub = lax.broadcasted_iota(jnp.int32, (8, 128), 0)
    tiles = [list(r) for r in tiles]
    full = (8, 128)
    piv = None
    for c in range(0, nrow, b):
        ltc, l0 = (base + c) // 128, (base + c) % 128
        rt0, s0 = c // 8, c % 8
        o = (c // b) % 2 * 8
        for lt in range(lt_n):
            scr[o : o + 8, 128 * lt : 128 * lt + 128] = tiles[rt0][lt]
        rows = [
            [
                jnp.broadcast_to(scr[o + s0 + s : o + s0 + s + 1, 128 * lt : 128 * lt + 128], full)
                for lt in range(lt_n)
            ]
            for s in range(b)
        ]
        cols = [
            [
                jnp.broadcast_to(tiles[rt][ltc][:, l0 + s : l0 + s + 1], full)
                for rt in range(rt_n)
            ]
            for s in range(b)
        ]
        if piv is None:
            piv = {
                (s, t): jnp.broadcast_to(rows[s][ltc][:, l0 + t : l0 + t + 1], full)
                for s in range(b)
                for t in range(s, b)
            }
        Q = inv_sym(piv, b)
        if c + b < nrow:
            nl, n0 = (base + c + b) // 128, (base + c + b) % 128
            rn, sn = (c + b) // 8, (c + b) % 8
            X = {
                (v, t): jnp.broadcast_to(rows[v][nl][:, n0 + t : n0 + t + 1], full)
                for v in range(b)
                for t in range(b)
            }
            nrows = [
                jnp.broadcast_to(tiles[rn][nl][sn + s : sn + s + 1, :], full) for s in range(b)
            ]
            QX = {
                (u, t): ssum(Q[u, v] * X[v, t] for v in range(b))
                for u in range(b)
                for t in range(b)
            }
            piv = {
                (s, t): jnp.broadcast_to(nrows[s][:, n0 + t : n0 + t + 1], full)
                - ssum(X[u, s] * QX[u, t] for u in range(b))
                for s in range(b)
                for t in range(s, b)
            }
        colm = jnp.logical_and(lane >= l0, lane < l0 + b)
        R = []
        for s in range(b):
            rr = []
            for lt in range(lt_n):
                acc = ssum(Q[s, t] * rows[t][lt] for t in range(b))
                if lt == ltc:
                    for t in range(b):
                        acc = jnp.where(lane == l0 + t, -Q[s, t], acc)
                rr.append(acc)
            R.append(rr)
        for rt in range(rt_n):
            for lt in range(lt_n):
                m = tiles[rt][lt]
                if lt == ltc:
                    m = jnp.where(colm, 0.0, m)
                m = m - ssum(cols[s][rt] * R[s][lt] for s in range(b))
                if rt == rt0:
                    for s in range(b):
                        m = jnp.where(sub == s0 + s, R[s][lt], m)
                tiles[rt][lt] = m
        for hook in hooks[c // b :: nrow // b]:
            hook()
    return tiles


def split3(x):
    h = x.astype(BF16)
    r = x - h.astype(F32)
    m = r.astype(BF16)
    return h, m, (r - m.astype(F32)).astype(BF16)


def split2(x):
    h = x.astype(BF16)
    return h, (x - h.astype(F32)).astype(BF16)


def panel(m_ref, scr, k, hooks=()):
    nb = PANEL
    lane = lax.broadcasted_iota(jnp.int32, (nb, 256), 1)
    cm = lax.broadcasted_iota(jnp.int32, (1, 128), 1)
    r0 = k * nb
    slab = m_ref[r0 : r0 + nb, 0:256]
    tiles = [
        [m_ref[r0 + 8 * rt : r0 + 8 * rt + 8, 128 * lt : 128 * lt + 128] for lt in range(4)]
        for rt in range(nb // 8)
    ]
    tiles = sweep_slab(tiles, r0, PIV, nb, scr, hooks)
    R = jnp.concatenate([jnp.concatenate(t, axis=1) for t in tiles], axis=0)
    left = jnp.where(jnp.logical_and(lane >= r0, lane < r0 + nb), 0.0, slab)
    lh, lm, ll = split3(left)
    rh, rm, rl = split3(R)
    la = jnp.concatenate([lh, lh, lm, lh, lm, ll], axis=0)
    ra = jnp.concatenate([rh, rm, rh, rl, rm, rh], axis=0)
    l0 = (r0 // 128) * 128
    here = jnp.logical_and(cm >= r0 - l0, cm < r0 - l0 + nb)

    def apply(a, z):
        u = lax.dot_general(la[:, a:z], ra, TN, preferred_element_type=F32)
        for lt in range(4):
            cur = m_ref[a:z, 128 * lt : 128 * lt + 128]
            if 128 * lt == l0:
                cur = jnp.where(here, 0.0, cur)
            m_ref[a:z, 128 * lt : 128 * lt + 128] = cur - u[:, 128 * lt : 128 * lt + 128]

    if r0 + nb < 256:
        apply(r0 + nb, r0 + 2 * nb)
    if r0 > 0:
        apply(0, r0)
    if r0 + 2 * nb < 256:
        apply(r0 + 2 * nb, 256)
    m_ref[r0 : r0 + nb, :] = R


dot = functools.partial(lax.dot_general, dimension_numbers=NN, preferred_element_type=F32)
exact = functools.partial(dot, precision=HI)
GRP = 4


def main_kernel(
    nlat,
    nlon,
    place,
    tiles_ref,
    radius_ref,
    rows_in,
    noise_ref,
    values_ref,
    var_ref,
    cells_ref,
    alat,
    alon,
    diff,
    edge_ref,
    ens,
    ext,
    out,
    rows_ref,
    x_ref,
    reg_ref,
    mid_ref,
    o_ref,
    cb_ref,
    m_ref,
    scr,
    st_ref,
    sth_ref,
    stl_ref,
    w_ref,
    wh_ref,
    wm_ref,
    wl_ref,
    g_ref,
    u_ref,
    v_ref,
    g3_ref,
    a2_ref,
    insem,
    outsem,
):
    l = place[0]
    n = place[1]
    loads = [
        pltpu.make_async_copy(src, x_ref.at[pl.ds(i, ni), pl.ds(j, nj)], insem.at[s])
        for s, (src, i, ni, j, nj) in enumerate(
            (
                (ens, 2, CLAT, 2, CLON),
                (ext.at[pl.ds(0, 2)], 0, 2, 0, CLON + 4),
                (ext.at[pl.ds(CLAT + 2, 2)], CLAT + 2, 2, 0, CLON + 4),
                (ext.at[pl.ds(2, CLAT), pl.ds(0, 2)], 2, CLAT, 0, 2),
                (ext.at[pl.ds(2, CLAT), pl.ds(CLON + 2, 2)], 2, CLAT, CLON + 2, 2),
            )
        )
    ]
    for c in loads:
        c.start()
    for b in range(NB):
        rows_ref[b] = rows_in[b]

    def derived(a, e, k):
        return (
            1.0 - jnp.abs(a) - jnp.abs(e) - 4.0 * k,
            jnp.maximum(a, 0.0) + k,
            k - jnp.minimum(a, 0.0),
            jnp.maximum(e, 0.0) + k,
            k - jnp.minimum(e, 0.0),
        )

    def spread_column(j, i0, i1):
        for f, d in enumerate(derived(alat[j], alon[j], diff[j])):
            for i in range(i0, i1):
                cb_ref[f, 1 + i, 1 + j] = jnp.broadcast_to(d[:, i : i + 1], (8, 128))

    def spread_edge(d):
        der = derived(edge_ref[d, 0], edge_ref[d, 1], edge_ref[d, 2])
        if d < 2:
            outside = (l == nlat - 1) if d == 0 else (l == 0)
            keep = jnp.where(outside, 0.0, 1.0)
        for f in range(5):
            w = der[f] * keep if d < 2 else der[f]
            for t in range(CLON if d < 2 else CLAT):
                line = jnp.broadcast_to(w[:, t : t + 1], (8, 128))
                if d == 0:
                    cb_ref[f, CLAT + 1, 1 + t] = line
                elif d == 1:
                    cb_ref[f, 0, 1 + t] = line
                elif d == 2:
                    cb_ref[f, 1 + t, CLON + 1] = line
                else:
                    cb_ref[f, 1 + t, 0] = line

    ri = lax.broadcasted_iota(jnp.int32, (256, 256), 0)
    ci = lax.broadcasted_iota(jnp.int32, (256, 256), 1)
    eye = ri == ci
    total_lon = float(CLON * nlon)

    def column(row):
        return jnp.sum(jnp.where(eye, row, 0.0), axis=1, keepdims=True)

    def where_obs(b):
        pos = lax.shift_right_logical(cells_ref[pl.ds(b, 1), :], 3)
        lat = tiles_ref[0, b] * CLAT + lax.shift_right_logical(pos, 4)
        lon = tiles_ref[1, b] * CLON + jnp.bitwise_and(pos, 15)
        return lat.astype(F32), lon.astype(F32)

    def lon_sq(gap):
        gap = jnp.abs(gap)
        gap = jnp.minimum(gap, total_lon - gap)
        return gap * gap

    def prologue(b):
        rows = rows_ref[b]
        spread = rows - jnp.mean(rows, axis=1, keepdims=True)
        var = var_ref[pl.ds(b, 1), :]
        cov = lax.dot_general(spread, spread, NT, precision=HI, preferred_element_type=F32)
        m_ref[:, 0:256] = cov * (1.0 / (MEM - 1)) + jnp.where(eye, var, 0.0)
        m_ref[:, 256:512] = (
            column(values_ref[pl.ds(b, 1), :])
            + column(jnp.sqrt(var)) * noise_ref[b]
            - rows
        )
        spread_t = jnp.transpose(spread) * (1.0 / (MEM - 1))
        st_ref[...] = spread_t
        sth_ref[...], stl_ref[...] = split2(spread_t)
        reach = radius_ref[b].astype(F32)
        inv_sq = 1.0 / (jnp.full((1, 256), 1.0, F32) * (reach * reach))
        obs_lat, obs_lon = where_obs(b)
        for j in range(CLON + 4):
            pos = lax.rem(n * CLON + j - 2 + CLON * nlon, CLON * nlon).astype(F32)
            v_ref[j] = jnp.broadcast_to(lon_sq(pos - obs_lon) * inv_sq, (8, 256))
        for i in range(CLAT + 4):
            gap = (l * CLAT + i - 2).astype(F32) - obs_lat
            u_ref[i] = jnp.broadcast_to(1.0 - gap * gap * inv_sq, (8, 256))
        return obs_lat, obs_lon, inv_sq

    def regress_rows(c, where):
        obs_lat, obs_lon, inv_sq = where
        r = rows_ref[c]
        mine_lat, mine_lon = where_obs(c)
        dlat = column(mine_lat) - obs_lat
        d2 = dlat * dlat + lon_sq(column(mine_lon) - obs_lon)
        taper = jnp.maximum(1.0 - d2 * inv_sq, 0.0)
        an = r - jnp.mean(r, axis=1, keepdims=True)
        g_ref[c] = exact(an, st_ref[...]) * (taper * taper)

    size = GRP * (CLON + 4) * LEV

    def adjust(i):
        at = pl.ds(GRP * i, GRP)
        x = x_ref[at].reshape(size, MEM)
        gh, gm, gl = split3(reg_ref[at].reshape(size, 256))
        wh, wm, wl = wh_ref[...], wm_ref[...], wl_ref[...]
        small = dot(gm, wm) + dot(gh, wl) + dot(gl, wh)
        x = x + (dot(gh, wh) + ((dot(gm, wh) + dot(gh, wm)) + small))
        x_ref[at] = x.reshape(GRP, CLON + 4, LEV, MEM)
        return x

    def adjust_steps(i):
        at = pl.ds(GRP * i, GRP)
        shape = (GRP, CLON + 4, LEV, MEM)

        def parts():
            g3_ref[0], g3_ref[1], g3_ref[2] = split3(reg_ref[at].reshape(size, 256))

        def term(a, w):
            x_ref[at] = x_ref[at] + dot(g3_ref[a], w[...]).reshape(shape)

        pairs = ((0, wh_ref), (1, wh_ref), (0, wm_ref), (1, wm_ref), (0, wl_ref), (2, wh_ref))
        return [parts] + [functools.partial(term, a, w) for a, w in pairs]

    def regress_steps(i):
        at = pl.ds(GRP * i, GRP)
        shape = (GRP, CLON + 4, LEV, 256)

        def parts():
            x = x_ref[at].reshape(size, MEM)
            a2_ref[0], a2_ref[1] = split2(x - jnp.mean(x, axis=1, keepdims=True))
            reg_ref[at] = dot(a2_ref[0], sth_ref[...]).reshape(shape)

        def second():
            reg_ref[at] = reg_ref[at] + dot(a2_ref[1], sth_ref[...]).reshape(shape)

        def third():
            reg = reg_ref[at] + dot(a2_ref[0], stl_ref[...]).reshape(shape)
            tap = jnp.maximum(u_ref[at][:, None] - v_ref[...][None], 0.0)
            reg_ref[at] = reg * (tap * tap)

        return [parts, second, third]

    def together(steps, count):
        cut = [len(steps) * q // count for q in range(count + 1)]

        def run(q):
            for f in steps[cut[q] : cut[q + 1]]:
                f()

        return [functools.partial(run, q) for q in range(count)]

    def keep_weights():
        weights = m_ref[:, 256:512]
        w_ref[...] = weights
        wh_ref[...], wm_ref[...], wl_ref[...] = split3(weights)

    where = prologue(0)
    for c in loads:
        c.wait()
    for k in range(8):
        steps = regress_steps(k) + (regress_steps(8) if k == 7 else [])
        hooks = together(steps, 8)
        for q in range(8):
            j = 2 * k + q // 4
            hooks.append(functools.partial(spread_column, j, 8 * (q % 4), 8 * (q % 4) + 8))
        panel(m_ref, scr, k, hooks)
        if k < 4:
            spread_edge(k)
        if k == 3:
            regress_rows(1, where)
        if k == 4:
            regress_rows(2, where)
    keep_weights()

    def batch(b, carry):
        rows_ref[b] = rows_ref[b] + exact(g_ref[b], w_ref[...])
        where = prologue(b)
        for k in range(8):
            steps = adjust_steps(k) + regress_steps(k)
            if k == 7:
                steps += adjust_steps(8) + regress_steps(8)
            panel(m_ref, scr, k, together(steps, 8))
            if k == 0:
                rows_ref[2] = rows_ref[2] + exact(g_ref[2], w_ref[...])
            if k == 3:
                regress_rows(2, where)
        keep_weights()
        return carry

    lax.fori_loop(1, NB, batch, 0)

    def last(i, carry):
        adjust(i)
        return carry

    lax.fori_loop(0, 9, last, 0)

    @pl.when(l == 0)
    def _():
        x_ref[0:2] = jnp.zeros((2, CLON + 4, LEV, MEM), F32)

    @pl.when(l == nlat - 1)
    def _():
        x_ref[CLAT + 2 : CLAT + 4] = jnp.zeros((2, CLON + 4, LEV, MEM), F32)

    def first(i, carry):
        for h in range(2):
            m = pl.ds(128 * h, 128)
            mid_ref[i, :, :, m] = (
                cb_ref[0, i] * x_ref[i + 1, 1:19, :, m]
                + cb_ref[1, i] * x_ref[i, 1:19, :, m]
                + cb_ref[2, i] * x_ref[i + 2, 1:19, :, m]
                + cb_ref[3, i] * x_ref[i + 1, 0:18, :, m]
                + cb_ref[4, i] * x_ref[i + 1, 2:20, :, m]
            )
        return carry

    lax.fori_loop(0, CLAT + 2, first, 0)

    def second(i, carry):
        for h in range(2):
            m = pl.ds(128 * h, 128)
            o_ref[i, :, :, m] = (
                cb_ref[0, i + 1, 1:17] * mid_ref[i + 1, 1:17, :, m]
                + cb_ref[1, i + 1, 1:17] * mid_ref[i, 1:17, :, m]
                + cb_ref[2, i + 1, 1:17] * mid_ref[i + 2, 1:17, :, m]
                + cb_ref[3, i + 1, 1:17] * mid_ref[i + 1, 0:16, :, m]
                + cb_ref[4, i + 1, 1:17] * mid_ref[i + 1, 2:18, :, m]
            )
        pltpu.make_async_copy(o_ref.at[i], out.at[i], outsem).start()
        return carry

    lax.fori_loop(0, CLAT, second, 0)
    pltpu.make_async_copy(o_ref, out, outsem).wait()


def main_call(nlat, nlon):
    dma = pltpu.SemaphoreType.DMA
    sq = lambda t: pltpu.VMEM((256, 256), t)
    return pl.pallas_call(
        functools.partial(main_kernel, nlat, nlon),
        out_shape=jax.ShapeDtypeStruct((CLAT, CLON, LEV, MEM), F32),
        in_specs=[pl.BlockSpec(memory_space=SM)] * 3
        + [pl.BlockSpec(memory_space=VM)] * 9
        + [pl.BlockSpec(memory_space=pl.ANY)] * 2,
        out_specs=pl.BlockSpec(memory_space=pl.ANY),
        scratch_shapes=[
            pltpu.VMEM((NB, NOBS, MEM), F32),
            pltpu.VMEM((CLAT + 4, CLON + 4, LEV, MEM), F32),
            pltpu.VMEM((CLAT + 4, CLON + 4, LEV, NOBS), F32),
            pltpu.VMEM((CLAT + 2, CLON + 2, LEV, MEM), F32),
            pltpu.VMEM((CLAT, CLON, LEV, MEM), F32),
            pltpu.VMEM((5, CLAT + 2, CLON + 2, LEV, 128), F32),
            pltpu.VMEM((256, 512), F32),
            pltpu.VMEM((16, 512), F32),
            sq(F32),
            sq(BF16),
            sq(BF16),
            sq(F32),
            sq(BF16),
            sq(BF16),
            sq(BF16),
            pltpu.VMEM((NB, 256, 256), F32),
            pltpu.VMEM((CLAT + 4, LEV, 256), F32),
            pltpu.VMEM((CLON + 4, LEV, 256), F32),
            pltpu.VMEM((3, GRP * (CLON + 4) * LEV, 256), BF16),
            pltpu.VMEM((2, GRP * (CLON + 4) * LEV, 256), BF16),
            dma((5,)),
            dma,
        ],
        compiler_params=pltpu.CompilerParams(vmem_limit_bytes=60 << 20),
        name="assimilate",
    )


def shards(
    nlat,
    nlon,
    ensemble,
    obs_values,
    obs_noise,
    obs_var,
    obs_cells,
    owner_tiles,
    radius,
    courant_lat,
    courant_lon,
    diffusivity,
):
    piece = NOBS // nlon
    dma = pltpu.SemaphoreType.DMA
    tiles = owner_tiles.T
    coefs = [jnp.transpose(c, (1, 2, 0)) for c in (courant_lat, courant_lon, diffusivity)]
    vm = pl.BlockSpec(memory_space=VM)
    sm = pl.BlockSpec(memory_space=SM)
    anym = pl.BlockSpec(memory_space=pl.ANY)
    rows, edges_in, place, ext = pl.pallas_call(
        functools.partial(exchange_kernel, nlat, nlon),
        out_shape=(
            jax.ShapeDtypeStruct((NB, NOBS, MEM), F32),
            jax.ShapeDtypeStruct((4, 3, LEV, 32), F32),
            jax.ShapeDtypeStruct((2,), jnp.int32),
            jax.ShapeDtypeStruct((CLAT + 4, CLON + 4, LEV, MEM), F32),
        ),
        in_specs=[sm, sm, anym, vm, vm, vm],
        out_specs=(vm, vm, sm, anym),
        scratch_shapes=[
            pltpu.VMEM((CLAT, CLON, LEV, MEM), F32),
            pltpu.VMEM((NB, NOBS, MEM), F32),
            pltpu.VMEM((4, 3, LEV, 32), F32),
            pltpu.VMEM((nlon - 1, NB, piece, MEM), F32),
            pltpu.VMEM((nlat - 1, NB, piece, MEM), F32),
            pltpu.VMEM((NB, piece, MEM), F32),
            pltpu.VMEM((NB, piece, MEM), F32),
            dma((2,)),
            dma((2,)),
            dma((2,)),
            dma((2,)),
            dma((2,)),
            dma((2,)),
            dma((8,)),
            dma((8,)),
            dma((4,)),
            dma((4,)),
            dma,
        ],
        compiler_params=pltpu.CompilerParams(
            collective_id=0, has_side_effects=True, vmem_limit_bytes=56 << 20
        ),
        name="exchange",
    )(tiles, obs_cells, ensemble, *coefs)

    return main_call(nlat, nlon)(
        place,
        tiles,
        radius,
        rows,
        obs_noise,
        obs_values,
        obs_var,
        obs_cells,
        *coefs,
        edges_in,
        ensemble,
        ext,
    )


def solution(mesh):
    nlat, nlon = mesh.shape["lat"], mesh.shape["lon"]
    tile = P("lat", "lon", None)
    return jax.shard_map(
        functools.partial(shards, nlat, nlon),
        mesh=mesh,
        in_specs=(P("lat", "lon", None, None),) + (P(),) * 6 + (tile,) * 3,
        out_specs=P("lat", "lon", None, None),
        check_vma=False,
    )
```

```python
import functools

import jax
import jax.numpy as jnp
from jax import lax
from jax.experimental import pallas as pl
from jax.experimental.pallas import tpu as pltpu
from jax.sharding import PartitionSpec as P

F32 = jnp.float32
BF16 = jnp.bfloat16
HI = lax.Precision.HIGHEST
MESH = pl.DeviceIdType.MESH
NN = (((1,), (0,)), ((), ()))
NT = (((1,), (1,)), ((), ()))
TN = (((0,), (0,)), ((), ()))

LEV = 8
NB = 3
CLAT = 32
CLON = 16
NOBS = 256
MEM = 256
PIV = 4
PANEL = 32
VM = pltpu.VMEM
SM = pltpu.SMEM


def exchange_kernel(
    nlat,
    nlon,
    tiles_ref,
    cells_ref,
    ens,
    alat,
    alon,
    diff,
    rows,
    edges_in,
    place,
    ext,
    state,
    picked,
    edges,
    got0,
    halves,
    got1,
    got2,
    part1,
    part2,
    s0,
    r0,
    s1,
    r1,
    s2,
    r2,
    s3,
    r3,
    s4,
    r4,
    hs,
    hr,
    es,
    er,
    loc,
):
    l = lax.axis_index("lat")
    n = lax.axis_index("lon")
    piece = NOBS // nlon
    half = NOBS // 2
    chips = nlon // 2
    core, chip = lax.rem(n, 2), n // 2
    twin = n + 1 - 2 * core
    keep = pl.ds(pl.multiple_of(core * half, half), half)
    give = pl.ds(pl.multiple_of((1 - core) * half, half), half)
    mine = pl.ds(pl.multiple_of(core * half + chip * piece, piece), piece)
    lm, lp = lax.rem(l + nlat - 1, nlat), lax.rem(l + 1, nlat)
    nm, np_ = lax.rem(n + nlon - 1, nlon), lax.rem(n + 1, nlon)

    load = pltpu.make_async_copy(ens, state, loc)
    load.start()
    bar = pltpu.get_barrier_semaphore()

    def greet_lon(r, carry):
        pl.semaphore_signal(bar, inc=1, device_id=(l, lax.rem(n + r, nlon)), device_id_type=MESH)
        return carry

    def greet_lat(r, carry):
        pl.semaphore_signal(bar, inc=1, device_id=(lax.rem(l + r, nlat), n), device_id_type=MESH)
        return carry

    lax.fori_loop(1, nlon, greet_lon, 0)
    lax.fori_loop(1, nlat, greet_lat, 0)
    for a in (lm, lp):
        for c in (nm, np_):
            pl.semaphore_signal(bar, inc=1, device_id=(a, c), device_id_type=MESH)
    pl.semaphore_wait(bar, nlon - 1 + nlat - 1 + 4)

    place[0] = l
    place[1] = n
    lane = lax.broadcasted_iota(jnp.int32, (LEV, 32), 1)
    for q, coef in enumerate((alat, alon, diff)):
        edges[2, q] = coef[0]
        edges[3, q] = coef[CLON - 1]
        for d, t in ((0, 0), (1, CLAT - 1)):
            line = jnp.zeros((LEV, 32), F32)
            for j in range(CLON):
                line = jnp.where(lane == j, coef[j, :, t : t + 1], line)
            edges[d, q] = line
    flat = state.reshape(CLAT * CLON * LEV, MEM)

    def pick(b):
        own = jnp.logical_and(tiles_ref[0, b] == l, tiles_ref[1, b] == n).astype(F32)

        def body(o, carry):
            for u in range(8):
                c = cells_ref[b, o * 8 + u]
                picked[b, pl.ds(o * 8 + u, 1), :] = flat[pl.ds(c, 1), :] * own
            return carry

        lax.fori_loop(0, NOBS // 8, body, 0)

    load.wait()

    groups = ((0, 1), (1, 2))

    def swap0(g):
        b0, nb = groups[g]
        return pltpu.make_async_remote_copy(
            src_ref=picked.at[pl.ds(b0, nb), give],
            dst_ref=got0.at[pl.ds(b0, nb)],
            send_sem=s0.at[g],
            recv_sem=r0.at[g],
            device_id=(l, twin),
            device_id_type=MESH,
        )

    def swap4(g):
        b0, nb = groups[g]
        return pltpu.make_async_remote_copy(
            src_ref=rows.at[pl.ds(b0, nb), keep],
            dst_ref=rows.at[pl.ds(b0, nb), keep],
            send_sem=s4.at[g],
            recv_sem=r4.at[g],
            device_id=(l, twin),
            device_id_type=MESH,
        )

    def send1(g):
        b0, nb = groups[g]
        halves[pl.ds(b0, nb)] = picked[pl.ds(b0, nb), keep, :] + got0[pl.ds(b0, nb)]

        def go(r, carry):
            peer = lax.rem(chip + r, chips)
            pltpu.make_async_remote_copy(
                src_ref=halves.at[pl.ds(b0, nb), pl.ds(peer * piece, piece)],
                dst_ref=got1.at[r - 1, pl.ds(b0, nb)],
                send_sem=s1.at[g],
                recv_sem=r1.at[g],
                device_id=(l, 2 * peer + core),
                device_id_type=MESH,
            ).start()
            return carry

        lax.fori_loop(1, chips, go, 0)

    def wait1(g):
        b0, nb = groups[g]
        full = got1.at[:, pl.ds(b0, nb)]
        pltpu.make_async_copy(full, full, r1.at[g]).wait()

    def send2(g):
        b0, nb = groups[g]
        tot = halves[pl.ds(b0, nb), pl.ds(pl.multiple_of(chip * piece, piece), piece), :]
        for i in range(chips - 1):
            tot = tot + got1[i, pl.ds(b0, nb)]
        part1[pl.ds(b0, nb)] = tot

        def go(r, carry):
            peer = lax.rem(l + r, nlat)
            pltpu.make_async_remote_copy(
                src_ref=part1.at[pl.ds(b0, nb)],
                dst_ref=got2.at[r - 1, pl.ds(b0, nb)],
                send_sem=s2.at[g],
                recv_sem=r2.at[g],
                device_id=(peer, n),
                device_id_type=MESH,
            ).start()
            return carry

        lax.fori_loop(1, nlat, go, 0)

    def wait2(g):
        b0, nb = groups[g]
        full = got2.at[:, pl.ds(b0, nb)]
        pltpu.make_async_copy(full, full, r2.at[g]).wait()

    def send3(g):
        b0, nb = groups[g]
        tot = part1[pl.ds(b0, nb)]
        for i in range(nlat - 1):
            tot = tot + got2[i, pl.ds(b0, nb)]
        part2[pl.ds(b0, nb)] = tot
        rows[pl.ds(b0, nb), mine, :] = tot

        def go(r, carry):
            peer = lax.rem(chip + r, chips)
            pltpu.make_async_remote_copy(
                src_ref=part2.at[pl.ds(b0, nb)],
                dst_ref=rows.at[pl.ds(b0, nb), mine],
                send_sem=s3.at[g],
                recv_sem=r3.at[g],
                device_id=(l, 2 * peer + core),
                device_id_type=MESH,
            ).start()
            return carry

        lax.fori_loop(1, chips, go, 0)

    def wait3(g):
        b0, nb = groups[g]
        full = rows.at[pl.ds(b0, nb), pl.ds(0, half - piece)]
        pltpu.make_async_copy(full, full, r3.at[g]).wait()

    firsts = [swap0(g) for g in range(2)]
    lasts = [swap4(g) for g in range(2)]
    pick(0)
    firsts[0].start()
    pick(1)
    firsts[0].wait_recv()
    send1(0)
    pick(2)
    firsts[1].start()
    moves = (
        ((lm, n), (0, 2, 0, CLON), (34, 2)),
        ((lp, n), (CLAT - 2, 2, 0, CLON), (0, 2)),
        ((l, nm), (0, CLAT, 0, 2), (2, 18)),
        ((l, np_), (0, CLAT, CLON - 2, 2), (2, 0)),
        ((lm, nm), (0, 1, 0, 1), (34, 18)),
        ((lm, np_), (0, 1, CLON - 1, 1), (34, 1)),
        ((lp, nm), (CLAT - 1, 1, 0, 1), (1, 18)),
        ((lp, np_), (CLAT - 1, 1, CLON - 1, 1), (1, 1)),
    )
    copies = []
    for i, (dev, (i0, ni, j0, nj), (di, dj)) in enumerate(moves):
        copies.append(
            pltpu.make_async_remote_copy(
                src_ref=ens.at[pl.ds(i0, ni), pl.ds(j0, nj)],
                dst_ref=ext.at[pl.ds(di, ni), pl.ds(dj, nj)],
                send_sem=hs.at[i],
                recv_sem=hr.at[i],
                device_id=dev,
                device_id_type=MESH,
            )
        )
        if i < 4:
            copies.append(
                pltpu.make_async_remote_copy(
                    src_ref=edges.at[i],
                    dst_ref=edges_in.at[i],
                    send_sem=es.at[i],
                    recv_sem=er.at[i],
                    device_id=dev,
                    device_id_type=MESH,
                )
            )
    for c in copies:
        c.start()

    wait1(0)
    send2(0)
    firsts[1].wait_recv()
    send1(1)
    wait2(0)
    send3(0)
    wait1(1)
    send2(1)
    wait2(1)
    send3(1)

    wait3(0)
    lasts[0].start()
    wait3(1)
    lasts[1].start()
    for c in lasts:
        c.wait_recv()
    for c in firsts + lasts:
        c.wait_send()
    for g in range(2):
        b0, nb = groups[g]
        src = halves.at[pl.ds(b0, nb), pl.ds(0, half - piece)]
        pltpu.make_async_copy(src, src, s1.at[g]).wait()
        full = got2.at[:, pl.ds(b0, nb)]
        pltpu.make_async_copy(full, full, s2.at[g]).wait()
        pltpu.make_async_copy(src, src, s3.at[g]).wait()
    for c in copies:
        c.wait()


def ssum(xs):
    xs = list(xs)
    while len(xs) > 1:
        xs = [xs[i] + xs[i + 1] if i + 1 < len(xs) else xs[i] for i in range(0, len(xs), 2)]
    return xs[0]


def inv_sym(p, b):
    if b == 1:
        return {(0, 0): 1.0 / p[0, 0]}
    if b == 2:
        a, c, d = p[0, 0], p[0, 1], p[1, 1]
        r = 1.0 / (a * d - c * c)
        off = -(c * r)
        return {(0, 0): d * r, (0, 1): off, (1, 0): off, (1, 1): a * r}
    h = b // 2
    hs = range(h)
    A = inv_sym({(s, t): p[s, t] for s in hs for t in range(s, h)}, h)
    B = {(s, t): p[s, h + t] for s in hs for t in hs}
    AB = {(s, t): ssum(A[s, u] * B[u, t] for u in hs) for s in hs for t in hs}
    S = {
        (s, t): p[h + s, h + t] - ssum(B[u, s] * AB[u, t] for u in hs)
        for s in hs
        for t in range(s, h)
    }
    Si = inv_sym(S, h)
    ABS = {(s, t): ssum(AB[s, u] * Si[u, t] for u in hs) for s in hs for t in hs}
    Q = {}
    for s in hs:
        for t in hs:
            Q[s, t] = A[s, t] + ssum(ABS[s, u] * AB[t, u] for u in hs)
            Q[s, h + t] = -ABS[s, t]
            Q[h + t, s] = Q[s, h + t]
            Q[h + s, h + t] = Si[s, t]
    return Q


def sweep_slab(tiles, base, b, nrow, scr, hooks=()):
    rt_n, lt_n = nrow // 8, len(tiles[0])
    lane = lax.broadcasted_iota(jnp.int32, (8, 128), 1)
    sub = lax.broadcasted_iota(jnp.int32, (8, 128), 0)
    tiles = [list(r) for r in tiles]
    full = (8, 128)
    piv = None
    for c in range(0, nrow, b):
        ltc, l0 = (base + c) // 128, (base + c) % 128
        rt0, s0 = c // 8, c % 8
        o = (c // b) % 2 * 8
        for lt in range(lt_n):
            scr[o : o + 8, 128 * lt : 128 * lt + 128] = tiles[rt0][lt]
        rows = [
            [
                jnp.broadcast_to(scr[o + s0 + s : o + s0 + s + 1, 128 * lt : 128 * lt + 128], full)
                for lt in range(lt_n)
            ]
            for s in range(b)
        ]
        cols = [
            [
                jnp.broadcast_to(tiles[rt][ltc][:, l0 + s : l0 + s + 1], full)
                for rt in range(rt_n)
            ]
            for s in range(b)
        ]
        if piv is None:
            piv = {
                (s, t): jnp.broadcast_to(rows[s][ltc][:, l0 + t : l0 + t + 1], full)
                for s in range(b)
                for t in range(s, b)
            }
        Q = inv_sym(piv, b)
        if c + b < nrow:
            nl, n0 = (base + c + b) // 128, (base + c + b) % 128
            rn, sn = (c + b) // 8, (c + b) % 8
            X = {
                (v, t): jnp.broadcast_to(rows[v][nl][:, n0 + t : n0 + t + 1], full)
                for v in range(b)
                for t in range(b)
            }
            nrows = [
                jnp.broadcast_to(tiles[rn][nl][sn + s : sn + s + 1, :], full) for s in range(b)
            ]
            QX = {
                (u, t): ssum(Q[u, v] * X[v, t] for v in range(b))
                for u in range(b)
                for t in range(b)
            }
            piv = {
                (s, t): jnp.broadcast_to(nrows[s][:, n0 + t : n0 + t + 1], full)
                - ssum(X[u, s] * QX[u, t] for u in range(b))
                for s in range(b)
                for t in range(s, b)
            }
        colm = jnp.logical_and(lane >= l0, lane < l0 + b)
        R = []
        for s in range(b):
            rr = []
            for lt in range(lt_n):
                acc = ssum(Q[s, t] * rows[t][lt] for t in range(b))
                if lt == ltc:
                    for t in range(b):
                        acc = jnp.where(lane == l0 + t, -Q[s, t], acc)
                rr.append(acc)
            R.append(rr)
        for rt in range(rt_n):
            for lt in range(lt_n):
                m = tiles[rt][lt]
                if lt == ltc:
                    m = jnp.where(colm, 0.0, m)
                m = m - ssum(cols[s][rt] * R[s][lt] for s in range(b))
                if rt == rt0:
                    for s in range(b):
                        m = jnp.where(sub == s0 + s, R[s][lt], m)
                tiles[rt][lt] = m
        for hook in hooks[c // b :: nrow // b]:
            hook()
    return tiles


def split3(x):
    h = x.astype(BF16)
    r = x - h.astype(F32)
    m = r.astype(BF16)
    return h, m, (r - m.astype(F32)).astype(BF16)


def split2(x):
    h = x.astype(BF16)
    return h, (x - h.astype(F32)).astype(BF16)


def panel(m_ref, scr, k, hooks=()):
    nb = PANEL
    lane = lax.broadcasted_iota(jnp.int32, (nb, 256), 1)
    cm = lax.broadcasted_iota(jnp.int32, (1, 128), 1)
    r0 = k * nb
    slab = m_ref[r0 : r0 + nb, 0:256]
    tiles = [
        [m_ref[r0 + 8 * rt : r0 + 8 * rt + 8, 128 * lt : 128 * lt + 128] for lt in range(4)]
        for rt in range(nb // 8)
    ]
    tiles = sweep_slab(tiles, r0, PIV, nb, scr, hooks)
    R = jnp.concatenate([jnp.concatenate(t, axis=1) for t in tiles], axis=0)
    left = jnp.where(jnp.logical_and(lane >= r0, lane < r0 + nb), 0.0, slab)
    lh, lm, ll = split3(left)
    rh, rm, rl = split3(R)
    la = jnp.concatenate([lh, lh, lm, lh, lm, ll], axis=0)
    ra = jnp.concatenate([rh, rm, rh, rl, rm, rh], axis=0)
    l0 = (r0 // 128) * 128
    here = jnp.logical_and(cm >= r0 - l0, cm < r0 - l0 + nb)

    def apply(a, z):
        u = lax.dot_general(la[:, a:z], ra, TN, preferred_element_type=F32)
        for lt in range(4):
            cur = m_ref[a:z, 128 * lt : 128 * lt + 128]
            if 128 * lt == l0:
                cur = jnp.where(here, 0.0, cur)
            m_ref[a:z, 128 * lt : 128 * lt + 128] = cur - u[:, 128 * lt : 128 * lt + 128]

    if r0 + nb < 256:
        apply(r0 + nb, r0 + 2 * nb)
    if r0 > 0:
        apply(0, r0)
    if r0 + 2 * nb < 256:
        apply(r0 + 2 * nb, 256)
    m_ref[r0 : r0 + nb, :] = R


dot = functools.partial(lax.dot_general, dimension_numbers=NN, preferred_element_type=F32)
exact = functools.partial(dot, precision=HI)
GRP = 4


def main_kernel(
    nlat,
    nlon,
    place,
    tiles_ref,
    radius_ref,
    rows_in,
    noise_ref,
    values_ref,
    var_ref,
    cells_ref,
    alat,
    alon,
    diff,
    edge_ref,
    ens,
    ext,
    out,
    rows_ref,
    x_ref,
    reg_ref,
    mid_ref,
    o_ref,
    cb_ref,
    m_ref,
    scr,
    st_ref,
    sth_ref,
    stl_ref,
    w_ref,
    wh_ref,
    wm_ref,
    wl_ref,
    g_ref,
    u_ref,
    v_ref,
    g3_ref,
    a2_ref,
    insem,
    outsem,
):
    l = place[0]
    n = place[1]
    loads = [
        pltpu.make_async_copy(src, x_ref.at[pl.ds(i, ni), pl.ds(j, nj)], insem.at[s])
        for s, (src, i, ni, j, nj) in enumerate(
            (
                (ens, 2, CLAT, 2, CLON),
                (ext.at[pl.ds(0, 2)], 0, 2, 0, CLON + 4),
                (ext.at[pl.ds(CLAT + 2, 2)], CLAT + 2, 2, 0, CLON + 4),
                (ext.at[pl.ds(2, CLAT), pl.ds(0, 2)], 2, CLAT, 0, 2),
                (ext.at[pl.ds(2, CLAT), pl.ds(CLON + 2, 2)], 2, CLAT, CLON + 2, 2),
            )
        )
    ]
    for c in loads:
        c.start()
    for b in range(NB):
        rows_ref[b] = rows_in[b]

    def derived(a, e, k):
        return (
            1.0 - jnp.abs(a) - jnp.abs(e) - 4.0 * k,
            jnp.maximum(a, 0.0) + k,
            k - jnp.minimum(a, 0.0),
            jnp.maximum(e, 0.0) + k,
            k - jnp.minimum(e, 0.0),
        )

    def spread_column(j, i0, i1):
        for f, d in enumerate(derived(alat[j], alon[j], diff[j])):
            for i in range(i0, i1):
                cb_ref[f, 1 + i, 1 + j] = jnp.broadcast_to(d[:, i : i + 1], (8, 128))

    def spread_edge(d):
        der = derived(edge_ref[d, 0], edge_ref[d, 1], edge_ref[d, 2])
        if d < 2:
            outside = (l == nlat - 1) if d == 0 else (l == 0)
            keep = jnp.where(outside, 0.0, 1.0)
        for f in range(5):
            w = der[f] * keep if d < 2 else der[f]
            for t in range(CLON if d < 2 else CLAT):
                line = jnp.broadcast_to(w[:, t : t + 1], (8, 128))
                if d == 0:
                    cb_ref[f, CLAT + 1, 1 + t] = line
                elif d == 1:
                    cb_ref[f, 0, 1 + t] = line
                elif d == 2:
                    cb_ref[f, 1 + t, CLON + 1] = line
                else:
                    cb_ref[f, 1 + t, 0] = line

    ri = lax.broadcasted_iota(jnp.int32, (256, 256), 0)
    ci = lax.broadcasted_iota(jnp.int32, (256, 256), 1)
    eye = ri == ci
    total_lon = float(CLON * nlon)

    def column(row):
        return jnp.sum(jnp.where(eye, row, 0.0), axis=1, keepdims=True)

    def where_obs(b):
        pos = lax.shift_right_logical(cells_ref[pl.ds(b, 1), :], 3)
        lat = tiles_ref[0, b] * CLAT + lax.shift_right_logical(pos, 4)
        lon = tiles_ref[1, b] * CLON + jnp.bitwise_and(pos, 15)
        return lat.astype(F32), lon.astype(F32)

    def lon_sq(gap):
        gap = jnp.abs(gap)
        gap = jnp.minimum(gap, total_lon - gap)
        return gap * gap

    def prologue(b):
        rows = rows_ref[b]
        spread = rows - jnp.mean(rows, axis=1, keepdims=True)
        var = var_ref[pl.ds(b, 1), :]
        cov = lax.dot_general(spread, spread, NT, precision=HI, preferred_element_type=F32)
        m_ref[:, 0:256] = cov * (1.0 / (MEM - 1)) + jnp.where(eye, var, 0.0)
        m_ref[:, 256:512] = (
            column(values_ref[pl.ds(b, 1), :])
            + column(jnp.sqrt(var)) * noise_ref[b]
            - rows
        )
        spread_t = jnp.transpose(spread) * (1.0 / (MEM - 1))
        st_ref[...] = spread_t
        sth_ref[...], stl_ref[...] = split2(spread_t)
        reach = radius_ref[b].astype(F32)
        inv_sq = 1.0 / (jnp.full((1, 256), 1.0, F32) * (reach * reach))
        obs_lat, obs_lon = where_obs(b)
        for j in range(CLON + 4):
            pos = lax.rem(n * CLON + j - 2 + CLON * nlon, CLON * nlon).astype(F32)
            v_ref[j] = jnp.broadcast_to(lon_sq(pos - obs_lon) * inv_sq, (8, 256))
        for i in range(CLAT + 4):
            gap = (l * CLAT + i - 2).astype(F32) - obs_lat
            u_ref[i] = jnp.broadcast_to(1.0 - gap * gap * inv_sq, (8, 256))
        return obs_lat, obs_lon, inv_sq

    def regress_rows(c, where):
        obs_lat, obs_lon, inv_sq = where
        r = rows_ref[c]
        mine_lat, mine_lon = where_obs(c)
        dlat = column(mine_lat) - obs_lat
        d2 = dlat * dlat + lon_sq(column(mine_lon) - obs_lon)
        taper = jnp.maximum(1.0 - d2 * inv_sq, 0.0)
        an = r - jnp.mean(r, axis=1, keepdims=True)
        g_ref[c] = exact(an, st_ref[...]) * (taper * taper)

    size = GRP * (CLON + 4) * LEV

    def adjust(i):
        at = pl.ds(GRP * i, GRP)
        x = x_ref[at].reshape(size, MEM)
        gh, gm, gl = split3(reg_ref[at].reshape(size, 256))
        wh, wm, wl = wh_ref[...], wm_ref[...], wl_ref[...]
        small = dot(gm, wm) + dot(gh, wl) + dot(gl, wh)
        x = x + (dot(gh, wh) + ((dot(gm, wh) + dot(gh, wm)) + small))
        x_ref[at] = x.reshape(GRP, CLON + 4, LEV, MEM)
        return x

    def adjust_steps(i):
        at = pl.ds(GRP * i, GRP)
        shape = (GRP, CLON + 4, LEV, MEM)

        def parts():
            g3_ref[0], g3_ref[1], g3_ref[2] = split3(reg_ref[at].reshape(size, 256))

        def term(a, w):
            x_ref[at] = x_ref[at] + dot(g3_ref[a], w[...]).reshape(shape)

        pairs = ((0, wh_ref), (1, wh_ref), (0, wm_ref), (1, wm_ref), (0, wl_ref), (2, wh_ref))
        return [parts] + [functools.partial(term, a, w) for a, w in pairs]

    def regress_steps(i):
        at = pl.ds(GRP * i, GRP)
        shape = (GRP, CLON + 4, LEV, 256)

        def parts():
            x = x_ref[at].reshape(size, MEM)
            a2_ref[0], a2_ref[1] = split2(x - jnp.mean(x, axis=1, keepdims=True))
            reg_ref[at] = dot(a2_ref[0], sth_ref[...]).reshape(shape)

        def second():
            reg_ref[at] = reg_ref[at] + dot(a2_ref[1], sth_ref[...]).reshape(shape)

        def third():
            reg = reg_ref[at] + dot(a2_ref[0], stl_ref[...]).reshape(shape)
            tap = jnp.maximum(u_ref[at][:, None] - v_ref[...][None], 0.0)
            reg_ref[at] = reg * (tap * tap)

        return [parts, second, third]

    def together(steps, count):
        cut = [len(steps) * q // count for q in range(count + 1)]

        def run(q):
            for f in steps[cut[q] : cut[q + 1]]:
                f()

        return [functools.partial(run, q) for q in range(count)]

    def keep_weights():
        weights = m_ref[:, 256:512]
        w_ref[...] = weights
        wh_ref[...], wm_ref[...], wl_ref[...] = split3(weights)

    where = prologue(0)
    for c in loads:
        c.wait()
    for k in range(8):
        steps = regress_steps(k) + (regress_steps(8) if k == 7 else [])
        hooks = together(steps, 8)
        for q in range(8):
            j = 2 * k + q // 4
            hooks.append(functools.partial(spread_column, j, 8 * (q % 4), 8 * (q % 4) + 8))
        panel(m_ref, scr, k, hooks)
        if k < 4:
            spread_edge(k)
        if k == 3:
            regress_rows(1, where)
        if k == 4:
            regress_rows(2, where)
    keep_weights()

    def batch(b, carry):
        rows_ref[b] = rows_ref[b] + exact(g_ref[b], w_ref[...])
        where = prologue(b)
        for k in range(8):
            steps = adjust_steps(k) + regress_steps(k)
            if k == 7:
                steps += adjust_steps(8) + regress_steps(8)
            panel(m_ref, scr, k, together(steps, 8))
            if k == 0:
                rows_ref[2] = rows_ref[2] + exact(g_ref[2], w_ref[...])
            if k == 3:
                regress_rows(2, where)
        keep_weights()
        return carry

    lax.fori_loop(1, NB, batch, 0)

    def last(i, carry):
        adjust(i)
        return carry

    lax.fori_loop(0, 9, last, 0)

    @pl.when(l == 0)
    def _():
        x_ref[0:2] = jnp.zeros((2, CLON + 4, LEV, MEM), F32)

    @pl.when(l == nlat - 1)
    def _():
        x_ref[CLAT + 2 : CLAT + 4] = jnp.zeros((2, CLON + 4, LEV, MEM), F32)

    def first(i, carry):
        for h in range(2):
            m = pl.ds(128 * h, 128)
            mid_ref[i, :, :, m] = (
                cb_ref[0, i] * x_ref[i + 1, 1:19, :, m]
                + cb_ref[1, i] * x_ref[i, 1:19, :, m]
                + cb_ref[2, i] * x_ref[i + 2, 1:19, :, m]
                + cb_ref[3, i] * x_ref[i + 1, 0:18, :, m]
                + cb_ref[4, i] * x_ref[i + 1, 2:20, :, m]
            )
        return carry

    lax.fori_loop(0, CLAT + 2, first, 0)

    def second(i, carry):
        for h in range(2):
            m = pl.ds(128 * h, 128)
            o_ref[i, :, :, m] = (
                cb_ref[0, i + 1, 1:17] * mid_ref[i + 1, 1:17, :, m]
                + cb_ref[1, i + 1, 1:17] * mid_ref[i, 1:17, :, m]
                + cb_ref[2, i + 1, 1:17] * mid_ref[i + 2, 1:17, :, m]
                + cb_ref[3, i + 1, 1:17] * mid_ref[i + 1, 0:16, :, m]
                + cb_ref[4, i + 1, 1:17] * mid_ref[i + 1, 2:18, :, m]
            )
        pltpu.make_async_copy(o_ref.at[i], out.at[i], outsem).start()
        return carry

    lax.fori_loop(0, CLAT, second, 0)
    pltpu.make_async_copy(o_ref, out, outsem).wait()


def main_call(nlat, nlon):
    dma = pltpu.SemaphoreType.DMA
    sq = lambda t: pltpu.VMEM((256, 256), t)
    return pl.pallas_call(
        functools.partial(main_kernel, nlat, nlon),
        out_shape=jax.ShapeDtypeStruct((CLAT, CLON, LEV, MEM), F32),
        in_specs=[pl.BlockSpec(memory_space=SM)] * 3
        + [pl.BlockSpec(memory_space=VM)] * 9
        + [pl.BlockSpec(memory_space=pl.ANY)] * 2,
        out_specs=pl.BlockSpec(memory_space=pl.ANY),
        scratch_shapes=[
            pltpu.VMEM((NB, NOBS, MEM), F32),
            pltpu.VMEM((CLAT + 4, CLON + 4, LEV, MEM), F32),
            pltpu.VMEM((CLAT + 4, CLON + 4, LEV, NOBS), F32),
            pltpu.VMEM((CLAT + 2, CLON + 2, LEV, MEM), F32),
            pltpu.VMEM((CLAT, CLON, LEV, MEM), F32),
            pltpu.VMEM((5, CLAT + 2, CLON + 2, LEV, 128), F32),
            pltpu.VMEM((256, 512), F32),
            pltpu.VMEM((16, 512), F32),
            sq(F32),
            sq(BF16),
            sq(BF16),
            sq(F32),
            sq(BF16),
            sq(BF16),
            sq(BF16),
            pltpu.VMEM((NB, 256, 256), F32),
            pltpu.VMEM((CLAT + 4, LEV, 256), F32),
            pltpu.VMEM((CLON + 4, LEV, 256), F32),
            pltpu.VMEM((3, GRP * (CLON + 4) * LEV, 256), BF16),
            pltpu.VMEM((2, GRP * (CLON + 4) * LEV, 256), BF16),
            dma((5,)),
            dma,
        ],
        compiler_params=pltpu.CompilerParams(vmem_limit_bytes=60 << 20),
        name="assimilate",
    )


def shards(
    nlat,
    nlon,
    ensemble,
    obs_values,
    obs_noise,
    obs_var,
    obs_cells,
    owner_tiles,
    radius,
    courant_lat,
    courant_lon,
    diffusivity,
):
    piece = NOBS // nlon
    dma = pltpu.SemaphoreType.DMA
    tiles = owner_tiles.T
    coefs = [jnp.transpose(c, (1, 2, 0)) for c in (courant_lat, courant_lon, diffusivity)]
    vm = pl.BlockSpec(memory_space=VM)
    sm = pl.BlockSpec(memory_space=SM)
    anym = pl.BlockSpec(memory_space=pl.ANY)
    rows, edges_in, place, ext = pl.pallas_call(
        functools.partial(exchange_kernel, nlat, nlon),
        out_shape=(
            jax.ShapeDtypeStruct((NB, NOBS, MEM), F32),
            jax.ShapeDtypeStruct((4, 3, LEV, 32), F32),
            jax.ShapeDtypeStruct((2,), jnp.int32),
            jax.ShapeDtypeStruct((CLAT + 4, CLON + 4, LEV, MEM), F32),
        ),
        in_specs=[sm, sm, anym, vm, vm, vm],
        out_specs=(vm, vm, sm, anym),
        scratch_shapes=[
            pltpu.VMEM((CLAT, CLON, LEV, MEM), F32),
            pltpu.VMEM((NB, NOBS, MEM), F32),
            pltpu.VMEM((4, 3, LEV, 32), F32),
            pltpu.VMEM((NB, NOBS // 2, MEM), F32),
            pltpu.VMEM((NB, NOBS // 2, MEM), F32),
            pltpu.VMEM((nlon // 2 - 1, NB, piece, MEM), F32),
            pltpu.VMEM((nlat - 1, NB, piece, MEM), F32),
            pltpu.VMEM((NB, piece, MEM), F32),
            pltpu.VMEM((NB, piece, MEM), F32),
            dma((2,)),
            dma((2,)),
            dma((2,)),
            dma((2,)),
            dma((2,)),
            dma((2,)),
            dma((2,)),
            dma((2,)),
            dma((2,)),
            dma((2,)),
            dma((8,)),
            dma((8,)),
            dma((4,)),
            dma((4,)),
            dma,
        ],
        compiler_params=pltpu.CompilerParams(
            collective_id=0, has_side_effects=True, vmem_limit_bytes=56 << 20
        ),
        name="exchange",
    )(tiles, obs_cells, ensemble, *coefs)

    return main_call(nlat, nlon)(
        place,
        tiles,
        radius,
        rows,
        obs_noise,
        obs_values,
        obs_var,
        obs_cells,
        *coefs,
        edges_in,
        ensemble,
        ext,
    )


def solution(mesh):
    nlat, nlon = mesh.shape["lat"], mesh.shape["lon"]
    tile = P("lat", "lon", None)
    return jax.shard_map(
        functools.partial(shards, nlat, nlon),
        mesh=mesh,
        in_specs=(P("lat", "lon", None, None),) + (P(),) * 6 + (tile,) * 3,
        out_specs=P("lat", "lon", None, None),
        check_vma=False,
    )
```
